128 devices in a mesh: dp: 8 (over y_lo, z), fsdp: 16 (over y_hi, x, core).
Axes of the slice: x: 4, y: 4 (y_hi: 2, y_lo: 2; y = y_hi * 2 + y_lo), z: 4, core: 2. Of those that a mesh axis runs over, the one named last changes fastest.
Arguments:
- img_emb: bfloat16 [16, 2560, 1152], P('fsdp', 'dp'), may hold values from -0.5 to 0.5
- txt_feat: bfloat16 [16, 2560, 1152], P('fsdp', 'dp'), may hold values from -0.405 to 0.405
- w_txt: float32 [1152, 1152], P('fsdp'), may hold values from -0.125 to 1.125
- t_log: float32 [1], replicated, may hold values from 1.6 to 2.4
- bias: float32 [1], replicated, may hold values from -4 to -2.5
Outputs:
- d_img_emb: bfloat16 [16, 2560, 1152], P('fsdp', 'dp')
- d_txt_feat: bfloat16 [16, 2560, 1152], P('fsdp', 'dp')
- d_w_txt: float32 [1152, 1152], P('fsdp')
The draws below stay inside these ranges and needn't reach their ends.
All inputs are finite; a program needn't handle non-finite values.
Results may differ from the reference program's by a relative error of at most 0.015.
Values may be sent and summed in bfloat16 or wider, within the bound.
No kernel may reach another device: no remote copies, remote signals or barrier semaphores. Data moves between devices by JAX's collectives and lax.ppermute only.
A program may use at most 128 MiB of HBM per device.

```python
import math
import jax
import jax.numpy as jnp
from jax import lax

D = 1152
E = 1152
TOK_DEV = 320
CONTRAST = 2560
GROUPS = 16
N_DP = 8


def text_rows(key):
    key = jax.random.fold_in(key, 11)
    normal_key = jax.random.fold_in(key, 0)
    perm_key = jax.random.fold_in(key, 2)
    shape_all = (GROUPS, CONTRAST, D)
    base_rows = jnp.clip(jax.random.normal(normal_key, shape_all, jnp.float32), -4.5, 4.5)
    owner_block = jax.random.permutation(perm_key, GROUPS)
    feature_block = jnp.arange(D) // (D // GROUPS)
    boost_factor = jnp.where(feature_block[None, :] == owner_block[:, None], 3.0, 1.0).astype(jnp.float32)
    return 0.03 * base_rows * boost_factor[:, None, :]


def image_rows(key):
    shared_text = text_rows(key)
    key = jax.random.fold_in(key, 5)
    noise_key = jax.random.fold_in(key, 0)
    pick_key = jax.random.fold_in(key, 2)
    reach_key = jax.random.fold_in(key, 3)
    index_key = jax.random.fold_in(key, 4)
    mix_key = jax.random.fold_in(key, 5)
    shape_all = (GROUPS, CONTRAST, E)
    noise_rows = jnp.clip(jax.random.normal(noise_key, shape_all, jnp.float32), -4.5, 4.5)
    noise_rows = 0.03 * noise_rows
    row_ids = jnp.arange(CONTRAST, dtype=jnp.int32)
    chosen = jax.random.randint(pick_key, (GROUPS, CONTRAST), 0, 4) == 0
    reach_blocks = jax.random.randint(reach_key, (GROUPS, CONTRAST), 2, N_DP - 1)
    slot_index = jax.random.randint(index_key, (GROUPS, CONTRAST), 0, TOK_DEV)
    partner = (row_ids[None, :] // TOK_DEV + reach_blocks) % N_DP * TOK_DEV + slot_index
    copied = jax.vmap(lambda rows, picks: rows[picks])(shared_text, partner)
    blend_factor = jax.random.uniform(mix_key, (GROUPS, CONTRAST, 1), jnp.float32, 0.2, 0.6)
    return jnp.where(chosen[:, :, None], copied + blend_factor * noise_rows, noise_rows)


def draw_txt_feat(key, part):
    values = text_rows(key)
    return values.astype(jnp.bfloat16)


def draw_img_emb(key, part):
    values = image_rows(key)
    return values.astype(jnp.bfloat16)


def draw_w_txt(key, part):
    key = jax.random.fold_in(key, 7)
    spread = jnp.clip(jax.random.normal(key, (D, E), jnp.float32), -4.0, 4.0)
    spread = jnp.clip(0.5 * spread / math.sqrt(D), -0.125, 0.125)
    return jnp.eye(D, E, dtype=jnp.float32) + spread


def setup_inputs(seed: int = 0) -> dict:
    key_list = jax.random.split(jax.random.key(seed), 6)
    return {
        "img_emb": draw_img_emb(jax.random.fold_in(key_list[5], 71), 0),
        "txt_feat": draw_txt_feat(jax.random.fold_in(key_list[5], 71), 0),
        "w_txt": draw_w_txt(jax.random.fold_in(key_list[5], 71), 0),
        "t_log": jnp.clip(jax.random.uniform(key_list[3], (1,), jnp.float32, 1.6, 2.4), 1.6, 2.4),
        "bias": jnp.clip(jax.random.uniform(key_list[4], (1,), jnp.float32, -4.0, -2.5), -4.0, -2.5),
    }


def normalize(latent):
    length = jnp.sqrt(lax.optimization_barrier(jnp.sum(latent * latent, axis=-1, keepdims=True)) + 1e-06)
    unit_rows = latent / length
    return (unit_rows, length, unit_rows.astype(jnp.bfloat16))

def project_back(grad_unit, unit_rows, length):
    inner = lax.optimization_barrier(jnp.sum(unit_rows * grad_unit, axis=-1, keepdims=True))
    return ((grad_unit - unit_rows * inner) / length).astype(jnp.bfloat16)

def block_sum(partials):
    rounded = partials.astype(jnp.bfloat16)
    rounded = lax.optimization_barrier(rounded)
    return lax.optimization_barrier(jnp.sum(rounded.astype(jnp.float32), axis=1))

def reference(img_emb, txt_feat, w_txt, t_log, bias):
    w_half = w_txt.astype(jnp.bfloat16)
    logit_scale = jnp.exp(t_log[0])
    logit_bias = bias[0]
    identity = jnp.eye(CONTRAST, dtype=jnp.float32)

    def per_group(inputs):
        img_rows, txt_rows = inputs
        u_img, s_img, n_img = normalize(img_rows.astype(jnp.float32))
        z_txt = jnp.dot(txt_rows, w_half, preferred_element_type=jnp.float32)
        u_txt, s_txt, n_txt = normalize(z_txt)
        logits = logit_scale * jnp.dot(n_img, n_txt.T, preferred_element_type=jnp.float32) + logit_bias
        grad_logit = (jax.nn.sigmoid(logits) - identity).astype(jnp.bfloat16)
        grad_wide = grad_logit.astype(jnp.float32)
        txt_blocks = n_txt.astype(jnp.float32).reshape(N_DP, TOK_DEV, E)
        img_blocks = n_img.astype(jnp.float32).reshape(N_DP, TOK_DEV, E)
        part_img = jnp.einsum('cnb,nbe->cne', grad_wide.reshape(CONTRAST, N_DP, TOK_DEV), txt_blocks)
        part_txt = jnp.einsum('nbc,nbe->cne', grad_wide.reshape(N_DP, TOK_DEV, CONTRAST), img_blocks)
        g_img = block_sum(logit_scale * part_img)
        g_txt = block_sum(logit_scale * part_txt)
        d_img = project_back(g_img, u_img, s_img)
        dz_txt = project_back(g_txt, u_txt, s_txt)
        d_txt = jnp.dot(dz_txt, w_half.T, preferred_element_type=jnp.float32).astype(jnp.bfloat16)
        weight_term = jnp.dot(txt_rows.T, dz_txt, preferred_element_type=jnp.float32)
        return (d_img, d_txt, weight_term)
    d_img, d_txt, terms = lax.map(per_group, (img_emb, txt_feat))
    return (d_img, d_txt, lax.optimization_barrier(jnp.sum(terms, axis=0)))
```

```python
import jax
import jax.numpy as jnp
from jax import lax
from jax.experimental import pallas as pl
from jax.experimental.pallas import tpu as pltpu
from jax.sharding import Mesh, PartitionSpec as P

BF = jnp.bfloat16
F32 = jnp.float32
MIB = 1024 * 1024
AXES = {"ylo": 2, "z": 4, "yhi": 2, "x": 4, "core": 2}

VM = pl.BlockSpec(memory_space=pltpu.VMEM)
SM = pl.BlockSpec(memory_space=pltpu.SMEM)


def shift(value, axis, step):
    n = AXES[axis]
    return lax.ppermute(value, axis, [(i, (i + step) % n) for i in range(n)])


def swap_far(value):
    pairs = [(a * 2 + b, (1 - a) * 2 + 1 - b) for a in range(2) for b in range(2)]
    return lax.ppermute(value, ("ylo", "yhi"), pairs)


def shaped(shape, dtype):
    return jax.ShapeDtypeStruct(shape, dtype)


def call(kernel, outs, specs, flops, nbytes, scratch=(), vmem=48):
    return pl.pallas_call(
        kernel,
        out_shape=outs,
        in_specs=specs,
        out_specs=[VM] * len(outs),
        scratch_shapes=list(scratch),
        compiler_params=pltpu.CompilerParams(vmem_limit_bytes=vmem * MIB),
        cost_estimate=pl.CostEstimate(flops=flops, bytes_accessed=nbytes, transcendentals=0),
    )


def row_length(rows):
    return jnp.sqrt(jnp.sum(rows * rows, axis=-1, keepdims=True) + 1e-06)


def project(grad, unit, length):
    inner = jnp.sum(unit * grad, axis=-1, keepdims=True)
    return (grad - unit * inner) / length


def prepare_kernel(img, w, n_img, w_half):
    w_half[...] = w[...].astype(BF)
    rows = img[...].astype(F32)
    n_img[...] = (rows / row_length(rows)).astype(BF)


def text_kernel(at, txt, txt_far, *refs):
    pieces, (w_full, z, n_txt, wide) = refs[:16], refs[16:]
    yhi, x, core = at[0], at[1], at[2]
    for flip_core in range(2):
        for flip_y in range(2):
            for back in range(4):
                y_of = yhi if flip_y == 0 else 1 - yhi
                c_of = core if flip_core == 0 else 1 - core
                owner = y_of * 8 + ((x + 4 - back) % 4) * 2 + c_of
                piece = pieces[flip_core * 8 + flip_y * 4 + back]
                start = pl.multiple_of(owner * 72, 8)
                wide[pl.ds(start, 72), :] = piece[...].astype(F32)
    w_full[...] = wide[...].astype(BF)
    head = w_full[...]
    for half, rows in enumerate((txt, txt_far)):
        out = jnp.dot(rows[...], head, preferred_element_type=F32)
        z[half] = out
        n_txt[half] = (out / row_length(out)).astype(BF)


def tile(scal, img_blk, txt_blk, diagonal):
    logits = scal[0] * lax.dot_general(
        img_blk, txt_blk, (((1,), (1,)), ((), ())), preferred_element_type=F32
    ) + scal[1]
    grad = jax.nn.sigmoid(logits)
    if diagonal:
        row_ids = lax.broadcasted_iota(jnp.int32, logits.shape, 0)
        col_ids = lax.broadcasted_iota(jnp.int32, logits.shape, 1)
        grad = grad - jnp.where(row_ids == col_ids, 1.0, 0.0)
    grad = grad.astype(BF)
    part = scal[0] * jnp.dot(grad, txt_blk, preferred_element_type=F32)
    back = lax.dot_general(
        grad, img_blk, (((0,), (0,)), ((), ())), preferred_element_type=F32
    )
    return part, back


def near_kernel(scal, n_own, n_a, n_b, n_txt, part_own, part_a, part_b, acc):
    txt_blk = n_txt[...].reshape(640, 1152)
    for step, (img_blk, part_ref) in enumerate(
        ((n_own, part_own), (n_a, part_a), (n_b, part_b))
    ):
        part, back = tile(scal, img_blk[...], txt_blk, step == 0)
        part_ref[...] = part.astype(BF)
        if step == 0:
            acc[...] = back
        else:
            acc[...] += back


def far_kernel(scal, n_c, n_txt, acc, z, part_c, g_own, g_far, dz):
    txt_blk = n_txt[...].reshape(640, 1152)
    part, back = tile(scal, n_c[...], txt_blk, False)
    part_c[...] = part.astype(BF)
    for half, out in enumerate((g_own, g_far)):
        rows = pl.ds(half * 320, 320)
        grad = scal[0] * (acc[rows, :] + back[half * 320 : half * 320 + 320])
        out[...] = grad.astype(BF)
        z_rows = z[half]
        length = row_length(z_rows)
        dz[rows, :] = project(grad, z_rows / length, length).astype(BF)


def weight_kernel(at, txt, txt_far, dz, mine, other, wide):
    core = at[2]
    for k in range(3):
        cols = pl.ds(k * 384, 384)
        total = None
        for half, rows in enumerate((txt, txt_far)):
            term = lax.dot_general(
                rows[:, cols],
                dz[pl.ds(half * 320, 320), :],
                (((0,), (0,)), ((), ())),
                preferred_element_type=F32,
            )
            total = term if total is None else total + term
        wide[cols, :] = total
    for j in range(8):
        a = pl.multiple_of((2 * j + core) * 72, 8)
        b = pl.multiple_of((2 * j + 1 - core) * 72, 8)
        mine[j] = wide[pl.ds(a, 72), :].astype(BF)
        other[j] = wide[pl.ds(b, 72), :].astype(BF)


def core_sum_kernel(at, mine, got, *outs):
    x = at[1]
    for r in range(4):
        owner = (x + r) % 4
        for h in range(2):
            j = h * 4 + owner
            outs[r][h] = (mine[j].astype(F32) + got[j].astype(F32)).astype(BF)


def x_sum_kernel(at, a, b, c, d, keep, send):
    yhi = at[0]
    for out, h in ((keep, yhi), (send, 1 - yhi)):
        total = (a[h].astype(F32) + b[h].astype(F32)) + (c[h].astype(F32) + d[h].astype(F32))
        out[...] = total.astype(BF)


def pair_sum_kernel(a, b, out):
    out[...] = (a[...].astype(F32) + b[...].astype(F32)).astype(BF)


def z_sum_kernel(a, b, c, d, out):
    out[...] = (a[...].astype(F32) + b[...].astype(F32)) + (c[...].astype(F32) + d[...].astype(F32))


def image_out_kernel(img, a, b, c, d, out):
    rows = img[...].astype(F32)
    length = row_length(rows)
    grad = (a[...].astype(F32) + b[...].astype(F32)) + (c[...].astype(F32) + d[...].astype(F32))
    out[...] = project(grad, rows / length, length).astype(BF)


def text_out_kernel(z, a, b, w_full, out):
    rows = z[0]
    length = row_length(rows)
    grad = a[...].astype(F32) + b[...].astype(F32)
    dz = project(grad, rows / length, length).astype(BF)
    out[...] = lax.dot_general(
        dz, w_full[...], (((1,), (1,)), ((), ())), preferred_element_type=F32
    ).astype(BF)


def on_device(img_emb, txt_feat, w_txt, t_log, bias):
    img, txt = img_emb[0], txt_feat[0]
    at = jnp.stack([lax.axis_index("yhi"), lax.axis_index("x"), lax.axis_index("core")]).astype(jnp.int32)
    scal = jnp.concatenate([jnp.exp(t_log), bias])
    block = shaped((320, 1152), BF)
    mac = 2 * 320 * 1152

    txt_far = shift(txt, "ylo", 1)
    n_img, w_half = call(
        prepare_kernel, [block, shaped((72, 1152), BF)], [VM] * 2, mac, 2 * MIB
    )(img, w_txt)

    w_y = swap_far(w_half)
    own = [w_half] + [shift(w_half, "x", s) for s in (1, 2, 3)]
    own += [w_y] + [shift(w_y, "x", s) for s in (1, 2, 3)]
    cross = [shift(p, "core", 1) for p in own]
    n_a = shift(n_img, "z", 1)
    n_b = shift(n_img, "z", -1)
    n_c = shift(n_img, "z", 2)

    w_full, z, n_txt = call(
        text_kernel,
        [shaped((1152, 1152), BF), shaped((2, 320, 1152), F32), shaped((2, 320, 1152), BF)],
        [SM] + [VM] * 18,
        640 * 1152 * 1152 * 2,
        10 * MIB,
        [pltpu.VMEM((1152, 1152), F32)],
    )(at, txt, txt_far, *own, *cross)

    part_own, part_a, part_b, acc = call(
        near_kernel,
        [block, block, block, shaped((640, 1152), F32)],
        [SM] + [VM] * 4,
        3 * 3 * 640 * mac,
        10 * MIB,
    )(scal, n_img, n_a, n_b, n_txt)
    got_a = shift(part_a, "z", -1)
    got_b = shift(part_b, "z", 1)

    part_c, g_own, g_far, dz = call(
        far_kernel,
        [block, block, block, shaped((640, 1152), BF)],
        [SM] + [VM] * 4,
        3 * 640 * mac,
        10 * MIB,
    )(scal, n_c, n_txt, acc, z)
    got_c = shift(part_c, "z", 2)
    g_got = shift(g_far, "ylo", 1)

    eight = shaped((8, 72, 1152), BF)
    mine, other = call(
        weight_kernel,
        [eight, eight],
        [SM] + [VM] * 3,
        640 * 1152 * 1152 * 2,
        6 * MIB,
        [pltpu.VMEM((1152, 1152), F32)],
    )(at, txt, txt_far, dz)
    got_core = shift(other, "core", 1)
    two = shaped((2, 72, 1152), BF)
    rel = call(core_sum_kernel, [two] * 4, [SM, VM, VM], MIB, 4 * MIB)(at, mine, got_core)
    x_got = [shift(rel[s], "x", s) for s in (1, 2, 3)]
    one = shaped((72, 1152), BF)
    keep, send = call(x_sum_kernel, [one, one], [SM] + [VM] * 4, MIB, 2 * MIB)(at, rel[0], *x_got)
    (pair,) = call(pair_sum_kernel, [one], [VM] * 2, MIB, MIB)(keep, swap_far(send))
    (quad,) = call(pair_sum_kernel, [one], [VM] * 2, MIB, MIB)(pair, shift(pair, "ylo", 1))
    (d_weight,) = call(z_sum_kernel, [shaped((72, 1152), F32)], [VM] * 4, MIB, MIB)(
        quad, shift(quad, "z", 2), shift(quad, "z", 1), shift(quad, "z", -1)
    )

    (d_img,) = call(image_out_kernel, [block], [VM] * 5, 10 * mac, 4 * MIB)(
        img, part_own, got_c, got_a, got_b
    )
    (d_feat,) = call(text_out_kernel, [block], [VM] * 4, 1152 * mac, 6 * MIB)(
        z, g_own, g_got, w_full
    )
    return (d_img[None], d_feat[None], d_weight)


def solution(mesh):
    fine = Mesh(mesh.devices.reshape(2, 4, 2, 4, 2), tuple(AXES))
    dp, fsdp = ("ylo", "z"), ("yhi", "x", "core")
    placed = (P(fsdp, dp, None), P(fsdp, dp, None), P(fsdp, None), P(), P())
    return jax.shard_map(
        on_device,
        mesh=fine,
        in_specs=placed,
        out_specs=(P(fsdp, dp, None), P(fsdp, dp, None), P(fsdp, None)),
        check_vma=False,
    )
```

```python
import jax
import jax.numpy as jnp
from jax import lax
from jax.experimental import pallas as pl
from jax.experimental.pallas import tpu as pltpu
from jax.sharding import Mesh, PartitionSpec as P

BF = jnp.bfloat16
F32 = jnp.float32
MIB = 1024 * 1024
AXES = {"ylo": 2, "z": 4, "yhi": 2, "x": 4, "core": 2}

VM = pl.BlockSpec(memory_space=pltpu.VMEM)
SM = pl.BlockSpec(memory_space=pltpu.SMEM)
ANY = pl.BlockSpec(memory_space=pl.ANY)


def shift(value, axis, step):
    n = AXES[axis]
    return lax.ppermute(value, axis, [(i, (i + step) % n) for i in range(n)])


def swap_far(value):
    pairs = [(a * 2 + b, (1 - a) * 2 + 1 - b) for a in range(2) for b in range(2)]
    return lax.ppermute(value, ("ylo", "yhi"), pairs)


def shaped(shape, dtype):
    return jax.ShapeDtypeStruct(shape, dtype)


def call(kernel, outs, specs, scratch=(), vmem=48, out_specs=None, flops=1024):
    return pl.pallas_call(
        kernel,
        out_shape=outs,
        in_specs=specs,
        out_specs=out_specs or [VM] * len(outs),
        scratch_shapes=list(scratch),
        compiler_params=pltpu.CompilerParams(vmem_limit_bytes=vmem * MIB),
        cost_estimate=pl.CostEstimate(flops=flops, bytes_accessed=1024, transcendentals=0),
    )


def inverse_length(rows):
    return 1.0 / jnp.sqrt(jnp.sum(rows * rows, axis=-1, keepdims=True) + 1e-06)


def project(grad, rows):
    inv = inverse_length(rows)
    unit = rows * inv
    inner = jnp.sum(unit * grad, axis=-1, keepdims=True)
    return (grad - unit * inner) * inv


def prepare_kernel(w, img, w_half, n_img):
    w_half[...] = w[...].astype(BF)
    rows = img[...].astype(F32)
    n_img[...] = (rows * inverse_length(rows)).astype(BF)


def pack_kernel(*refs):
    pieces, out, sems = refs[:7], refs[7], refs[8]
    copies = [pltpu.make_async_copy(p, out.at[k], sems.at[k]) for k, p in enumerate(pieces)]
    for c in copies:
        c.start()
    for c in copies:
        c.wait()


def text_kernel(at, near_core, far_core, near_last, far_last, txt, txt_far, w_full, z, n_txt, mine, other, rows, sems):
    copies = [
        pltpu.make_async_copy(near_core, mine.at[pl.ds(0, 7)], sems.at[0]),
        pltpu.make_async_copy(far_core, other.at[pl.ds(0, 7)], sems.at[1]),
        pltpu.make_async_copy(near_last, mine.at[7], sems.at[2]),
        pltpu.make_async_copy(far_last, other.at[7], sems.at[3]),
        pltpu.make_async_copy(txt, rows.at[pl.ds(0, 320)], sems.at[4]),
        pltpu.make_async_copy(txt_far, rows.at[pl.ds(320, 320)], sems.at[5]),
    ]
    for c in copies:
        c.start()
    for c in copies[:4]:
        c.wait()
    yhi, x, core = at[0], at[1], at[2]
    for k in range(8):
        y_of = yhi if k < 4 else 1 - yhi
        owner = y_of * 4 + (x + 4 - (0, 1, 3, 2)[k % 4]) % 4
        a, b = mine[k].astype(F32), other[k].astype(F32)
        first = jnp.where(core == 0, a, b)
        second = jnp.where(core == 0, b, a)
        pair = jnp.concatenate([first, second], axis=0).astype(BF)
        w_full[pl.ds(pl.multiple_of(owner * 144, 16), 144), :] = pair
    for c in copies[4:]:
        c.wait()
    out = jnp.dot(rows[...], w_full[...], preferred_element_type=F32)
    z[...] = out
    n_txt[...] = (out * inverse_length(out)).astype(BF)


def logit_gradient(scal, img_rows, txt_rows):
    logits = scal[0] * lax.dot_general(
        img_rows, txt_rows, (((1,), (1,)), ((), ())), preferred_element_type=F32
    ) + scal[1]
    return 1.0 / (1.0 + jnp.exp(-logits))


def near_kernel(scal, n_own, n_a, n_b, n_txt, grad, acc, rows):
    rows[pl.ds(0, 320), :] = n_own[...]
    rows[pl.ds(320, 320), :] = n_a[...]
    rows[pl.ds(640, 320), :] = n_b[...]
    g = logit_gradient(scal, rows[...], n_txt[...])
    row_ids = lax.broadcasted_iota(jnp.int32, g.shape, 0)
    col_ids = lax.broadcasted_iota(jnp.int32, g.shape, 1)
    g = g - jnp.where((row_ids == col_ids) & (row_ids < 320), 1.0, 0.0)
    grad[...] = g.astype(BF)
    acc[...] = lax.dot_general(
        grad[...], rows[...], (((0,), (0,)), ((), ())), preferred_element_type=F32
    )


def far_kernel(at, scal, n_c0, n_c1, n_txt, acc, z, txt, txt_far, grad, g_own, g_far, mine, other, rows, feat, wide):
    rows[pl.ds(0, 160), :] = n_c0[...]
    rows[pl.ds(160, 160), :] = n_c1[...]
    feat[pl.ds(0, 320), :] = txt[...]
    feat[pl.ds(320, 320), :] = txt_far[...]
    grad[...] = logit_gradient(scal, rows[...], n_txt[...]).astype(BF)
    total = scal[0] * (
        acc[...]
        + lax.dot_general(grad[...], rows[...], (((0,), (0,)), ((), ())), preferred_element_type=F32)
    )
    g_own[...] = total[:320].astype(BF)
    g_far[...] = total[320:].astype(BF)
    dz = project(total, z[...]).astype(BF)
    wide[...] = lax.dot_general(
        feat[...], dz, (((0,), (0,)), ((), ())), preferred_element_type=F32
    )
    core = at[2]
    for j in range(8):
        a = pl.multiple_of((2 * j + core) * 72, 8)
        b = pl.multiple_of((2 * j + 1 - core) * 72, 8)
        mine[j] = wide[pl.ds(a, 72), :].astype(BF)
        other[j] = wide[pl.ds(b, 72), :].astype(BF)


def part_kernel(scal, grad, grad_c, n_txt, part_a, part_b, part_c):
    out = scal[0] * jnp.dot(grad[pl.ds(320, 640), :], n_txt[...], preferred_element_type=F32)
    part_a[...] = out[:320].astype(BF)
    part_b[...] = out[320:].astype(BF)
    part_c[...] = (scal[0] * jnp.dot(grad_c[...], n_txt[...], preferred_element_type=F32)).astype(BF)


def part_own_kernel(scal, grad, n_txt, part_own):
    part_own[...] = (
        scal[0] * jnp.dot(grad[pl.ds(0, 320), :], n_txt[...], preferred_element_type=F32)
    ).astype(BF)


def core_sum_kernel(at, mine, got, own, up, far_h, far_y, down):
    x = at[1]
    for r, outs in enumerate(
        ((own.at[0], own.at[1]), (up.at[0], up.at[1]), (far_h, far_y), (down.at[0], down.at[1]))
    ):
        for h in range(2):
            j = h * 4 + (x + r) % 4
            outs[h][...] = (mine[j].astype(F32) + got[j].astype(F32)).astype(BF)


def pass_kernel(up, got_h, down, got_y, up_out, down_out):
    up_out[0] = (up[0].astype(F32) + got_h[...].astype(F32)).astype(BF)
    up_out[1] = up[1]
    down_out[0] = down[0]
    down_out[1] = (down[1].astype(F32) + got_y[...].astype(F32)).astype(BF)


def x_sum_kernel(at, a, b, c, keep, send):
    yhi = at[0]
    for out, h in ((keep, yhi), (send, 1 - yhi)):
        out[...] = (a[h].astype(F32) + (b[h].astype(F32) + c[h].astype(F32))).astype(BF)


def quad_sum_kernel(a, b, c, d, out):
    total = (a[...].astype(F32) + b[...].astype(F32)) + (c[...].astype(F32) + d[...].astype(F32))
    out[...] = total.astype(out.dtype)


def image_out_kernel(img, a, b, c, d, out):
    grad = (a[...].astype(F32) + b[...].astype(F32)) + (c[...].astype(F32) + d[...].astype(F32))
    out[...] = project(grad, img[...].astype(F32)).astype(BF)


def text_out_kernel(z, a, b, w_full, out):
    grad = a[...].astype(F32) + b[...].astype(F32)
    dz = project(grad, z[pl.ds(0, 320), :]).astype(BF)
    out[...] = lax.dot_general(
        dz, w_full[...], (((1,), (1,)), ((), ())), preferred_element_type=F32
    ).astype(BF)


def apart(step, *args):
    outs = jax.eval_shape(step, *args)
    return lax.cond(
        lax.axis_index("z") < AXES["z"],
        step,
        lambda *_: tuple(jnp.zeros(o.shape, o.dtype) for o in outs),
        *args,
    )


BLOCK = shaped((320, 1152), BF)


def stack_of(*lead):
    return shaped((*lead, 72, 1152), BF)


def gather_head(w_h):
    hold = lax.optimization_barrier
    w_y, h_a = swap_far(w_h), shift(w_h, "x", 1)
    w_h, w_y, h_a = hold((w_h, w_y, h_a))
    h_b, y_a = shift(w_h, "x", -1), shift(w_y, "x", 1)
    w_y, h_a, h_b, y_a = hold((w_y, h_a, h_b, y_a))
    y_b, h_c = shift(w_y, "x", -1), shift(h_a, "x", 1)
    y_b, h_c = hold((y_b, h_c))
    y_c = shift(y_b, "x", -1)
    (near_core,) = call(
        pack_kernel, [stack_of(7)], [ANY] * 7, [pltpu.SemaphoreType.DMA((7,))], out_specs=[ANY]
    )(w_h, h_a, h_b, h_c, w_y, y_a, y_b)
    return near_core, shift(near_core, "core", 1), y_c, shift(y_c, "core", 1)


def reduce_x(at, mine, got_core, scal, grad, n_txt):
    rel = call(core_sum_kernel, [stack_of(2), stack_of(2), stack_of(), stack_of(), stack_of(2)], [SM, VM, VM])(
        at, mine, got_core
    )
    own, up, far_h, far_y, down = rel
    up, down = call(pass_kernel, [stack_of(2)] * 2, [VM] * 4)(
        up, shift(far_h, "x", 1), down, shift(far_y, "x", -1)
    )
    keep, send = call(x_sum_kernel, [stack_of()] * 2, [SM] + [VM] * 3)(
        at, own, shift(up, "x", 1), shift(down, "x", -1)
    )
    (part_own,) = call(part_own_kernel, [BLOCK], [SM] + [VM] * 2, flops=1 << 30)(scal, grad, n_txt)
    return keep, send, part_own


def reduce_yz(keep, send, z, g_own, g_got, w_full):
    (quad,) = call(quad_sum_kernel, [stack_of()], [VM] * 4)(
        keep, shift(keep, "ylo", 1), swap_far(send), shift(send, "yhi", 1)
    )
    (d_weight,) = call(quad_sum_kernel, [shaped((72, 1152), F32)], [VM] * 4)(
        quad, shift(quad, "z", 2), shift(quad, "z", 1), shift(quad, "z", -1)
    )
    (d_feat,) = call(text_out_kernel, [BLOCK], [VM] * 4, flops=1 << 31)(z, g_own, g_got, w_full)
    return d_weight, d_feat


def on_device(img_emb, txt_feat, w_txt, t_log, bias):
    img, txt = img_emb[0], txt_feat[0]
    at = jnp.stack([lax.axis_index("yhi"), lax.axis_index("x"), lax.axis_index("core")]).astype(jnp.int32)
    scal = jnp.concatenate([jnp.exp(t_log), bias])
    block = BLOCK

    txt_far = shift(txt, "ylo", 1)
    w_h, n_img = call(prepare_kernel, [stack_of(), block], [VM] * 2)(w_txt, img)
    n_a, n_b = shift(n_img, "z", 1), shift(n_img, "z", -1)
    head = apart(gather_head, w_h)
    head, n_a, n_b, txt_far = lax.optimization_barrier((head, n_a, n_b, txt_far))
    n_c0, n_c1 = shift(n_a[:160], "z", 1), shift(n_b[160:], "z", -1)

    w_full, z, n_txt = call(
        text_kernel,
        [shaped((1152, 1152), BF), shaped((640, 1152), F32), shaped((640, 1152), BF)],
        [SM] + [ANY] * 6,
        [
            pltpu.VMEM((8, 72, 1152), BF),
            pltpu.VMEM((8, 72, 1152), BF),
            pltpu.VMEM((640, 1152), BF),
            pltpu.SemaphoreType.DMA((6,)),
        ],
    )(at, *head, txt, txt_far)

    grad, acc = call(
        near_kernel,
        [shaped((960, 640), BF), shaped((640, 1152), F32)],
        [SM] + [VM] * 4,
        [pltpu.VMEM((960, 1152), BF)],
    )(scal, n_img, n_a, n_b, n_txt)
    grad_c, g_own, g_far, mine, other = call(
        far_kernel,
        [shaped((320, 640), BF), block, block, stack_of(8), stack_of(8)],
        [SM, SM] + [VM] * 7,
        [pltpu.VMEM((320, 1152), BF), pltpu.VMEM((640, 1152), BF), pltpu.VMEM((1152, 1152), F32)],
    )(at, scal, n_c0, n_c1, n_txt, acc, z, txt, txt_far)

    got_core = shift(other, "core", 1)
    g_got = shift(g_far, "ylo", 1)
    part_a, part_b, part_c = call(part_kernel, [block] * 3, [SM] + [VM] * 3)(
        scal, grad, grad_c, n_txt
    )
    got_a, got_b = shift(part_a, "z", -1), shift(part_b, "z", 1)
    keep, send, part_own = apart(reduce_x, at, mine, got_core, scal, grad, n_txt)
    keep, send, g_got, got_a, got_b, part_c = lax.optimization_barrier(
        (keep, send, g_got, got_a, got_b, part_c)
    )
    got_c = shift(part_c, "z", 2)
    d_weight, d_feat = apart(reduce_yz, keep, send, z, g_own, g_got, w_full)
    d_weight, got_c = lax.optimization_barrier((d_weight, got_c))

    (d_img,) = call(image_out_kernel, [block], [VM] * 5)(img, part_own, got_c, got_a, got_b)
    return (d_img[None], d_feat[None], d_weight)


def solution(mesh):
    fine = Mesh(mesh.devices.reshape(2, 4, 2, 4, 2), tuple(AXES))
    dp, fsdp = ("ylo", "z"), ("yhi", "x", "core")
    placed = (P(fsdp, dp, None), P(fsdp, dp, None), P(fsdp, None), P(), P())
    return jax.shard_map(
        on_device,
        mesh=fine,
        in_specs=placed,
        out_specs=(P(fsdp, dp, None), P(fsdp, dp, None), P(fsdp, None)),
        check_vma=False,
    )
```

```python
import jax
import jax.numpy as jnp
from jax import lax
from jax.experimental import pallas as pl
from jax.experimental.pallas import tpu as pltpu
from jax.sharding import Mesh, PartitionSpec as P

BF = jnp.bfloat16
F32 = jnp.float32
MIB = 1024 * 1024
AXES = {"ylo": 2, "z": 4, "yhi": 2, "x": 4, "core": 2}

VM = pl.BlockSpec(memory_space=pltpu.VMEM)
SM = pl.BlockSpec(memory_space=pltpu.SMEM)
ANY = pl.BlockSpec(memory_space=pl.ANY)


def shift(value, axis, step):
    n = AXES[axis]
    return lax.ppermute(value, axis, [(i, (i + step) % n) for i in range(n)])


def swap_far(value):
    pairs = [(a * 2 + b, (1 - a) * 2 + 1 - b) for a in range(2) for b in range(2)]
    return lax.ppermute(value, ("ylo", "yhi"), pairs)


def shaped(shape, dtype):
    return jax.ShapeDtypeStruct(shape, dtype)


def call(kernel, outs, specs, scratch=(), vmem=48, out_specs=None, flops=1024):
    return pl.pallas_call(
        kernel,
        out_shape=outs,
        in_specs=specs,
        out_specs=out_specs or [VM] * len(outs),
        scratch_shapes=list(scratch),
        compiler_params=pltpu.CompilerParams(vmem_limit_bytes=vmem * MIB),
        cost_estimate=pl.CostEstimate(flops=flops, bytes_accessed=1024, transcendentals=0),
    )


def inverse_length(rows):
    return 1.0 / jnp.sqrt(jnp.sum(rows * rows, axis=-1, keepdims=True) + 1e-06)


def project(grad, rows):
    inv = inverse_length(rows)
    unit = rows * inv
    inner = jnp.sum(unit * grad, axis=-1, keepdims=True)
    return (grad - unit * inner) * inv


def half_kernel(w, out):
    half = w[...].astype(BF)
    for k in range(8):
        out[k] = half


def unit_kernel(img, first, second):
    for at, out in ((0, first), (160, second)):
        rows = img[pl.ds(at, 160), :].astype(F32)
        out[...] = (rows * inverse_length(rows)).astype(BF)


def text_kernel(at, near_core, far_core, txt, txt_far, w_full, z, n_txt, mine, other, rows, sems):
    copies = [
        pltpu.make_async_copy(near_core, mine, sems.at[0]),
        pltpu.make_async_copy(far_core, other, sems.at[1]),
        pltpu.make_async_copy(txt, rows.at[pl.ds(0, 320)], sems.at[2]),
        pltpu.make_async_copy(txt_far, rows.at[pl.ds(320, 320)], sems.at[3]),
    ]
    for c in copies:
        c.start()
    for c in copies[:2]:
        c.wait()
    core = at[1]
    for k in range(8):
        a, b = mine[k].astype(F32), other[k].astype(F32)
        first = jnp.where(core == 0, a, b)
        second = jnp.where(core == 0, b, a)
        w_full[pl.ds(k * 144, 144), :] = jnp.concatenate([first, second], axis=0).astype(BF)
    for c in copies[2:]:
        c.wait()
    out = jnp.dot(rows[...], w_full[...], preferred_element_type=F32)
    z[...] = out
    n_txt[...] = (out * inverse_length(out)).astype(BF)


def logit_gradient(scal, img_rows, txt_rows):
    logits = scal[0] * lax.dot_general(
        img_rows, txt_rows, (((1,), (1,)), ((), ())), preferred_element_type=F32
    ) + scal[1]
    return 1.0 / (1.0 + jnp.exp(-logits))


def near_kernel(scal, n_own0, n_own1, n_a0, n_a1, n_b0, n_b1, n_txt, grad, acc, rows):
    for k, part in enumerate((n_own0, n_own1, n_a0, n_a1, n_b0, n_b1)):
        rows[pl.ds(k * 160, 160), :] = part[...]
    g = logit_gradient(scal, rows[...], n_txt[...])
    row_ids = lax.broadcasted_iota(jnp.int32, g.shape, 0)
    col_ids = lax.broadcasted_iota(jnp.int32, g.shape, 1)
    g = g - jnp.where((row_ids == col_ids) & (row_ids < 320), 1.0, 0.0)
    grad[...] = g.astype(BF)
    acc[...] = lax.dot_general(
        grad[...], rows[...], (((0,), (0,)), ((), ())), preferred_element_type=F32
    )


def far_kernel(at, scal, n_c0, n_c1, n_txt, acc, z, txt, txt_far, grad, g_own, g_far, mine, other, rows, feat, wide):
    rows[pl.ds(0, 160), :] = n_c0[...]
    rows[pl.ds(160, 160), :] = n_c1[...]
    feat[pl.ds(0, 320), :] = txt[...]
    feat[pl.ds(320, 320), :] = txt_far[...]
    grad[...] = logit_gradient(scal, rows[...], n_txt[...]).astype(BF)
    total = scal[0] * (
        acc[...]
        + lax.dot_general(grad[...], rows[...], (((0,), (0,)), ((), ())), preferred_element_type=F32)
    )
    g_own[...] = total[:320].astype(BF)
    g_far[...] = total[320:].astype(BF)
    dz = project(total, z[...]).astype(BF)
    wide[...] = lax.dot_general(
        feat[...], dz, (((0,), (0,)), ((), ())), preferred_element_type=F32
    )
    core = at[1]
    for j in range(8):
        a = pl.multiple_of((2 * j + core) * 72, 8)
        b = pl.multiple_of((2 * j + 1 - core) * 72, 8)
        mine[j] = wide[pl.ds(a, 72), :].astype(BF)
        other[j] = wide[pl.ds(b, 72), :].astype(BF)


def part_kernel(scal, grad, grad_c, n_txt, part_a, part_b, part_c):
    out = scal[0] * jnp.dot(grad[pl.ds(320, 640), :], n_txt[...], preferred_element_type=F32)
    part_a[...] = out[:320].astype(BF)
    part_b[...] = out[320:].astype(BF)
    part_c[...] = (scal[0] * jnp.dot(grad_c[...], n_txt[...], preferred_element_type=F32)).astype(BF)


def part_own_kernel(scal, grad, n_txt, part_own):
    part_own[...] = (
        scal[0] * jnp.dot(grad[pl.ds(0, 320), :], n_txt[...], preferred_element_type=F32)
    ).astype(BF)


def core_sum_kernel(a, b, out):
    out[...] = (a[...].astype(F32) + b[...].astype(F32)).astype(BF)


def plane_sum_kernel(got, out):
    out[...] = jnp.sum(got[...].astype(F32), axis=0).astype(BF)


def quad_sum_kernel(a, b, c, d, out):
    total = (a[...].astype(F32) + b[...].astype(F32)) + (c[...].astype(F32) + d[...].astype(F32))
    out[...] = total.astype(out.dtype)


def image_out_kernel(img, a, b, c, d, out):
    grad = (a[...].astype(F32) + b[...].astype(F32)) + (c[...].astype(F32) + d[...].astype(F32))
    out[...] = project(grad, img[...].astype(F32)).astype(BF)


def text_out_kernel(z, a, b, w_full, out):
    grad = a[...].astype(F32) + b[...].astype(F32)
    dz = project(grad, z[pl.ds(0, 320), :]).astype(BF)
    out[...] = lax.dot_general(
        dz, w_full[...], (((1,), (1,)), ((), ())), preferred_element_type=F32
    ).astype(BF)


def exchange_plane(value):
    groups = [
        [(ylo ^ yhi) * 8 + yhi * 4 + x for yhi in range(2) for x in range(4)] for ylo in range(2)
    ]
    return lax.all_to_all(
        value, ("ylo", "yhi", "x"), split_axis=0, concat_axis=0, axis_index_groups=groups, tiled=True
    )


BLOCK = shaped((320, 1152), BF)


def stack_of(*lead):
    return shaped((*lead, 72, 1152), BF)


def on_device(img_emb, txt_feat, w_txt, t_log, bias):
    img, txt = img_emb[0], txt_feat[0]
    at = jnp.stack([lax.axis_index("yhi"), lax.axis_index("core")]).astype(jnp.int32)
    scal = jnp.concatenate([jnp.exp(t_log), bias])
    block = BLOCK

    txt_far = shift(txt, "ylo", 1)
    (pieces,) = call(half_kernel, [stack_of(8)], [VM])(w_txt)
    img_a, img_b = shift(img, "z", 1), shift(img, "z", -1)
    near_core, img_a, img_b, txt_far = lax.optimization_barrier(
        (exchange_plane(pieces), img_a, img_b, txt_far)
    )
    far_core = shift(near_core, "core", 1)
    half = shaped((160, 1152), BF)
    n_a = call(unit_kernel, [half, half], [VM])(img_a)
    n_b = call(unit_kernel, [half, half], [VM])(img_b)
    n_c = shift(n_a[0], "z", 1), shift(n_b[1], "z", -1)
    n_own = call(unit_kernel, [half, half], [VM])(img)

    w_full, z, n_txt = call(
        text_kernel,
        [shaped((1152, 1152), BF), shaped((640, 1152), F32), shaped((640, 1152), BF)],
        [SM] + [ANY] * 4,
        [
            pltpu.VMEM((8, 72, 1152), BF),
            pltpu.VMEM((8, 72, 1152), BF),
            pltpu.VMEM((640, 1152), BF),
            pltpu.SemaphoreType.DMA((4,)),
        ],
    )(at, near_core, far_core, txt, txt_far)

    grad, acc = call(
        near_kernel,
        [shaped((960, 640), BF), shaped((640, 1152), F32)],
        [SM] + [VM] * 7,
        [pltpu.VMEM((960, 1152), BF)],
    )(scal, *n_own, *n_a, *n_b, n_txt)
    grad_c, g_own, g_far, mine, other = call(
        far_kernel,
        [shaped((320, 640), BF), block, block, stack_of(8), stack_of(8)],
        [SM, SM] + [VM] * 7,
        [pltpu.VMEM((320, 1152), BF), pltpu.VMEM((640, 1152), BF), pltpu.VMEM((1152, 1152), F32)],
    )(at, scal, *n_c, n_txt, acc, z, txt, txt_far)

    got_core = shift(other, "core", 1)
    g_got = shift(g_far, "ylo", 1)
    part_a, part_b, part_c = call(part_kernel, [block] * 3, [SM] + [VM] * 3)(
        scal, grad, grad_c, n_txt
    )
    got_a, got_b = shift(part_a, "z", -1), shift(part_b, "z", 1)
    got_c = shift(part_c, "z", 2)
    (both,) = call(core_sum_kernel, [stack_of(8)], [VM] * 2)(mine, got_core)
    (one,) = call(plane_sum_kernel, [stack_of()], [VM])(exchange_plane(both))
    (pair,) = call(core_sum_kernel, [stack_of()], [VM] * 2)(one, shift(one, "ylo", 1))
    got_a, got_b, got_c, g_got, pair = lax.optimization_barrier((got_a, got_b, got_c, g_got, pair))
    (part_own,) = call(part_own_kernel, [block], [SM] + [VM] * 2, flops=1 << 30)(scal, grad, n_txt)
    (d_feat,) = call(text_out_kernel, [block], [VM] * 4, flops=1 << 31)(z, g_own, g_got, w_full)
    (d_img,) = call(image_out_kernel, [block], [VM] * 5, flops=1 << 30)(img, part_own, got_c, got_a, got_b)
    (d_weight,) = call(quad_sum_kernel, [shaped((72, 1152), F32)], [VM] * 4)(
        pair, shift(pair, "z", 2), shift(pair, "z", 1), shift(pair, "z", -1)
    )
    return (d_img[None], d_feat[None], d_weight)


def solution(mesh):
    fine = Mesh(mesh.devices.reshape(2, 4, 2, 4, 2), tuple(AXES))
    dp, fsdp = ("ylo", "z"), ("yhi", "x", "core")
    placed = (P(fsdp, dp, None), P(fsdp, dp, None), P(fsdp, None), P(), P())
    return jax.shard_map(
        on_device,
        mesh=fine,
        in_specs=placed,
        out_specs=(P(fsdp, dp, None), P(fsdp, dp, None), P(fsdp, None)),
        check_vma=False,
    )
```

```python
import jax
import jax.numpy as jnp
from jax import lax
from jax.experimental import pallas as pl
from jax.experimental.pallas import tpu as pltpu
from jax.sharding import Mesh, PartitionSpec as P

BF = jnp.bfloat16
F32 = jnp.float32
MIB = 1024 * 1024
AXES = {"ylo": 2, "z": 4, "yhi": 2, "x": 4, "core": 2}

VM = pl.BlockSpec(memory_space=pltpu.VMEM)
SM = pl.BlockSpec(memory_space=pltpu.SMEM)
ANY = pl.BlockSpec(memory_space=pl.ANY)


def shift(value, axis, step):
    n = AXES[axis]
    return lax.ppermute(value, axis, [(i, (i + step) % n) for i in range(n)])


def swap_far(value):
    pairs = [(a * 2 + b, (1 - a) * 2 + 1 - b) for a in range(2) for b in range(2)]
    return lax.ppermute(value, ("ylo", "yhi"), pairs)


def shaped(shape, dtype):
    return jax.ShapeDtypeStruct(shape, dtype)


def call(kernel, outs, specs, scratch=(), vmem=48, out_specs=None, flops=1024):
    return pl.pallas_call(
        kernel,
        out_shape=outs,
        in_specs=specs,
        out_specs=out_specs or [VM] * len(outs),
        scratch_shapes=list(scratch),
        compiler_params=pltpu.CompilerParams(vmem_limit_bytes=vmem * MIB),
        cost_estimate=pl.CostEstimate(flops=flops, bytes_accessed=1024, transcendentals=0),
    )


def inverse_length(rows):
    return 1.0 / jnp.sqrt(jnp.sum(rows * rows, axis=-1, keepdims=True) + 1e-06)


def project(grad, rows):
    inv = inverse_length(rows)
    unit = rows * inv
    inner = jnp.sum(unit * grad, axis=-1, keepdims=True)
    return (grad - unit * inner) * inv


def prepare_kernel(w, img, w_half, n_img):
    w_half[...] = w[...].astype(BF)
    rows = img[...].astype(F32)
    n_img[...] = (rows * inverse_length(rows)).astype(BF)


def pack_kernel(*refs):
    pieces, out, sems = refs[:-2], refs[-2], refs[-1]
    copies = [pltpu.make_async_copy(p, out.at[k], sems.at[k]) for k, p in enumerate(pieces)]
    for c in copies:
        c.start()
    for c in copies:
        c.wait()


def pack(*pieces):
    n = len(pieces)
    (out,) = call(
        pack_kernel, [stack_of(n)], [ANY] * n, [pltpu.SemaphoreType.DMA((n,))], out_specs=[ANY]
    )(*pieces)
    return out


def text_kernel(at, near5, far5, near3, far3, txt, txt_far, w_full, z, n_txt, mine, other, rows, sems):
    copies = [
        pltpu.make_async_copy(near5, mine.at[pl.ds(0, 5)], sems.at[0]),
        pltpu.make_async_copy(far5, other.at[pl.ds(0, 5)], sems.at[1]),
        pltpu.make_async_copy(near3, mine.at[pl.ds(5, 3)], sems.at[2]),
        pltpu.make_async_copy(far3, other.at[pl.ds(5, 3)], sems.at[3]),
        pltpu.make_async_copy(txt, rows.at[pl.ds(0, 320)], sems.at[4]),
        pltpu.make_async_copy(txt_far, rows.at[pl.ds(320, 320)], sems.at[5]),
    ]
    for c in copies:
        c.start()
    for c in copies[:4]:
        c.wait()
    yhi, x, core = at[0], at[1], at[2]
    for k in range(8):
        y_of = yhi if k < 4 else 1 - yhi
        owner = y_of * 4 + (x + 4 - (0, 1, 3, 2)[k % 4]) % 4
        a, b = mine[k].astype(F32), other[k].astype(F32)
        first = jnp.where(core == 0, a, b)
        second = jnp.where(core == 0, b, a)
        pair = jnp.concatenate([first, second], axis=0).astype(BF)
        w_full[pl.ds(pl.multiple_of(owner * 144, 16), 144), :] = pair
    for c in copies[4:]:
        c.wait()
    out = jnp.dot(rows[...], w_full[...], preferred_element_type=F32)
    z[...] = out
    n_txt[...] = (out * inverse_length(out)).astype(BF)


def logit_gradient(scal, img_rows, txt_rows):
    logits = scal[0] * lax.dot_general(
        img_rows, txt_rows, (((1,), (1,)), ((), ())), preferred_element_type=F32
    ) + scal[1]
    return 1.0 / (1.0 + jnp.exp(-logits))


def own_kernel(scal, n_img, n_txt, grad, acc):
    g = logit_gradient(scal, n_img[...], n_txt[...])
    row_ids = lax.broadcasted_iota(jnp.int32, g.shape, 0)
    col_ids = lax.broadcasted_iota(jnp.int32, g.shape, 1)
    grad[...] = (g - jnp.where(row_ids == col_ids, 1.0, 0.0)).astype(BF)
    acc[...] = lax.dot_general(
        grad[...], n_img[...], (((0,), (0,)), ((), ())), preferred_element_type=F32
    )


def rest_kernel(at, scal, n_all, n_txt, acc, z, txt, txt_far, grad, g_own, g_far, mine, other, rows, feat, wide, sems):
    copies = [
        pltpu.make_async_copy(
            n_all.at[pl.ds(pl.multiple_of((at[3] + k) % 4 * 320, 320), 320)],
            rows.at[pl.ds((k - 1) * 320, 320)],
            sems.at[k - 1],
        )
        for k in (1, 2, 3)
    ]
    copies += [
        pltpu.make_async_copy(txt, feat.at[pl.ds(0, 320)], sems.at[3]),
        pltpu.make_async_copy(txt_far, feat.at[pl.ds(320, 320)], sems.at[4]),
    ]
    for c in copies:
        c.start()
    for c in copies:
        c.wait()
    grad[...] = logit_gradient(scal, rows[...], n_txt[...]).astype(BF)
    total = scal[0] * (
        acc[...]
        + lax.dot_general(grad[...], rows[...], (((0,), (0,)), ((), ())), preferred_element_type=F32)
    )
    g_own[...] = total[:320].astype(BF)
    g_far[...] = total[320:].astype(BF)
    dz = project(total, z[...]).astype(BF)
    wide[...] = lax.dot_general(
        feat[...], dz, (((0,), (0,)), ((), ())), preferred_element_type=F32
    )
    core = at[2]
    for j in range(8):
        a = pl.multiple_of((2 * j + core) * 72, 8)
        b = pl.multiple_of((2 * j + 1 - core) * 72, 8)
        mine[j] = wide[pl.ds(a, 72), :].astype(BF)
        other[j] = wide[pl.ds(b, 72), :].astype(BF)


def part_kernel(at, scal, grad_own, grad, n_txt, parts):
    for k in range(4):
        g = grad_own[...] if k == 0 else grad[pl.ds((k - 1) * 320, 320), :]
        out = scal[0] * jnp.dot(g, n_txt[...], preferred_element_type=F32)
        parts[pl.ds(pl.multiple_of((at[3] + k) % 4 * 320, 320), 320), :] = out.astype(BF)


def core_sum_kernel(at, mine, got, *outs):
    for r, out in enumerate(outs):
        for h in range(2):
            j = h * 4 + (at[1] + r) % 4
            out[h] = (mine[j].astype(F32) + got[j].astype(F32)).astype(BF)


def x_sum_kernel(at, a, b, c, d, keep, send):
    for out, h in ((keep, at[0]), (send, 1 - at[0])):
        total = (a[h].astype(F32) + b[h].astype(F32)) + (c[h].astype(F32) + d[h].astype(F32))
        out[...] = total.astype(BF)


def pair_sum_kernel(a, b, out):
    out[...] = (a[...].astype(F32) + b[...].astype(F32)).astype(BF)


def quad_sum_kernel(a, b, c, d, out):
    total = (a[...].astype(F32) + b[...].astype(F32)) + (c[...].astype(F32) + d[...].astype(F32))
    out[...] = total.astype(out.dtype)


def image_out_kernel(img, grad, out):
    out[...] = project(grad[...].astype(F32), img[...].astype(F32)).astype(BF)


def text_out_kernel(z, a, b, w_full, out):
    grad = a[...].astype(F32) + b[...].astype(F32)
    dz = project(grad, z[pl.ds(0, 320), :]).astype(BF)
    out[...] = lax.dot_general(
        dz, w_full[...], (((1,), (1,)), ((), ())), preferred_element_type=F32
    ).astype(BF)


def apart(step, *args):
    outs = jax.eval_shape(step, *args)
    return lax.cond(
        lax.axis_index("z") < AXES["z"],
        step,
        lambda *_: tuple(jnp.zeros(o.shape, o.dtype) for o in outs),
        *args,
    )


BLOCK = shaped((320, 1152), BF)


def stack_of(*lead):
    return shaped((*lead, 72, 1152), BF)


def gather_head(w_h):
    w_y = swap_far(w_h)
    h = [shift(w_h, "x", s) for s in (1, 3, 2)]
    y = [shift(w_y, "x", s) for s in (1, 3, 2)]
    near5, near3 = pack(w_h, *h, w_y), pack(*y)
    return near5, shift(near5, "core", 1), near3, shift(near3, "core", 1)


def swap_and_parts(other, at, scal, grad_own, grad, n_txt):
    (parts,) = call(
        part_kernel, [shaped((1280, 1152), BF)], [SM, SM] + [VM] * 3, flops=1 << 31
    )(at, scal, grad_own, grad, n_txt)
    return shift(other, "core", 1), parts


def on_device(img_emb, txt_feat, w_txt, t_log, bias):
    img, txt = img_emb[0], txt_feat[0]
    at = jnp.stack([lax.axis_index(a) for a in ("yhi", "x", "core", "z")]).astype(jnp.int32)
    scal = jnp.concatenate([jnp.exp(t_log), bias])

    txt_far = shift(txt, "ylo", 1)
    w_h, n_img = call(prepare_kernel, [stack_of(), BLOCK], [VM] * 2)(w_txt, img)
    n_all = lax.all_gather(n_img, "z", axis=0, tiled=True)
    head = apart(gather_head, w_h)
    head, txt_far = lax.optimization_barrier((head, txt_far))

    w_full, z, n_txt = call(
        text_kernel,
        [shaped((1152, 1152), BF), shaped((640, 1152), F32), shaped((640, 1152), BF)],
        [SM] + [ANY] * 6,
        [
            pltpu.VMEM((8, 72, 1152), BF),
            pltpu.VMEM((8, 72, 1152), BF),
            pltpu.VMEM((640, 1152), BF),
            pltpu.SemaphoreType.DMA((6,)),
        ],
    )(at, *head, txt, txt_far)
    grad_own, acc = call(
        own_kernel, [shaped((320, 640), BF), shaped((640, 1152), F32)], [SM] + [VM] * 2
    )(scal, n_img, n_txt)
    n_all, acc = lax.optimization_barrier((n_all, acc))
    grad, g_own, g_far, mine, other = call(
        rest_kernel,
        [shaped((960, 640), BF), BLOCK, BLOCK, stack_of(8), stack_of(8)],
        [SM, SM, ANY, VM, VM, VM, ANY, ANY],
        [
            pltpu.VMEM((960, 1152), BF),
            pltpu.VMEM((640, 1152), BF),
            pltpu.VMEM((1152, 1152), F32),
            pltpu.SemaphoreType.DMA((5,)),
        ],
    )(at, scal, n_all, n_txt, acc, z, txt, txt_far)

    got_core, parts = apart(swap_and_parts, other, at, scal, grad_own, grad, n_txt)
    g_img = lax.psum_scatter(parts, "z", scatter_dimension=0, tiled=True)
    rel = call(core_sum_kernel, [stack_of(2)] * 4, [SM, VM, VM])(at, mine, got_core)
    g_got = shift(g_far, "ylo", 1)
    keep, send = call(x_sum_kernel, [stack_of()] * 2, [SM] + [VM] * 4)(
        at, rel[0], *[shift(rel[s], "x", s) for s in (1, 2, 3)]
    )
    (pair,) = call(pair_sum_kernel, [stack_of()], [VM] * 2)(keep, swap_far(send))
    (quad,) = call(pair_sum_kernel, [stack_of()], [VM] * 2)(pair, shift(pair, "ylo", 1))
    (d_feat,) = call(text_out_kernel, [BLOCK], [VM] * 4, flops=1 << 31)(z, g_own, g_got, w_full)
    (d_img,) = call(image_out_kernel, [BLOCK], [VM] * 2, flops=1 << 30)(img, g_img)
    (d_weight,) = call(quad_sum_kernel, [shaped((72, 1152), F32)], [VM] * 4)(
        quad, shift(quad, "z", 2), shift(quad, "z", 1), shift(quad, "z", -1)
    )
    return (d_img[None], d_feat[None], d_weight)


def solution(mesh):
    fine = Mesh(mesh.devices.reshape(2, 4, 2, 4, 2), tuple(AXES))
    dp, fsdp = ("ylo", "z"), ("yhi", "x", "core")
    placed = (P(fsdp, dp, None), P(fsdp, dp, None), P(fsdp, None), P(), P())
    return jax.shard_map(
        on_device,
        mesh=fine,
        in_specs=placed,
        out_specs=(P(fsdp, dp, None), P(fsdp, dp, None), P(fsdp, None)),
        check_vma=False,
    )
```

```python
import functools

import jax
import jax.numpy as jnp
from jax import lax
from jax.experimental import pallas as pl
from jax.experimental.pallas import tpu as pltpu
from jax.sharding import Mesh, PartitionSpec as P

BF = jnp.bfloat16
F32 = jnp.float32
MIB = 1024 * 1024
EARLY = 768
TEXT_MIB = 16
MAIN_MIB = 26
AXES = {"ylo": 2, "z": 4, "yhi": 2, "x": 4, "core": 2}

VM = pl.BlockSpec(memory_space=pltpu.VMEM)
SM = pl.BlockSpec(memory_space=pltpu.SMEM)
ANY = pl.BlockSpec(memory_space=pl.ANY)


def shift(value, axis, step):
    n = AXES[axis]
    return lax.ppermute(value, axis, [(i, (i + step) % n) for i in range(n)])


def swap_far(value):
    pairs = [(a * 2 + b, (1 - a) * 2 + 1 - b) for a in range(2) for b in range(2)]
    return lax.ppermute(value, ("ylo", "yhi"), pairs)


def shaped(shape, dtype):
    return jax.ShapeDtypeStruct(shape, dtype)


def call(kernel, outs, specs, scratch=(), vmem=10, out_specs=None, flops=1024):
    return pl.pallas_call(
        kernel,
        out_shape=outs,
        in_specs=specs,
        out_specs=out_specs or [VM] * len(outs),
        scratch_shapes=list(scratch),
        compiler_params=pltpu.CompilerParams(vmem_limit_bytes=vmem * MIB),
        cost_estimate=pl.CostEstimate(flops=flops, bytes_accessed=1024, transcendentals=0),
    )


def inverse_length(rows):
    return 1.0 / jnp.sqrt(jnp.sum(rows * rows, axis=-1, keepdims=True) + 1e-06)


def project(grad, rows):
    inv = inverse_length(rows)
    unit = rows * inv
    inner = jnp.sum(unit * grad, axis=-1, keepdims=True)
    return (grad - unit * inner) * inv


def half_kernel(w, w_half):
    w_half[...] = w[...].astype(BF)


def repeat_kernel(at, w_h, w_y, out):
    for k in range(4):
        out[k, at[0]] = w_h[...]
        out[k, 1 - at[0]] = w_y[...]


def unit_kernel(img, _, n_img):
    rows = img[...].astype(F32)
    n_img[...] = (rows * inverse_length(rows)).astype(BF)


def text_kernel(at, near, far, txt, txt_far, w_full, z, n_txt, mine, other, rows, sems):
    copies = [
        pltpu.make_async_copy(near, mine, sems.at[0]),
        pltpu.make_async_copy(far, other, sems.at[1]),
        pltpu.make_async_copy(txt, rows.at[pl.ds(0, 320)], sems.at[2]),
        pltpu.make_async_copy(txt_far, rows.at[pl.ds(320, 320)], sems.at[3]),
    ]
    for c in copies:
        c.start()
    for c in copies[:2]:
        c.wait()
    core = at[2]
    for x in range(4):
        for h in range(2):
            a, b = mine[x, h].astype(F32), other[x, h].astype(F32)
            first = jnp.where(core == 0, a, b)
            second = jnp.where(core == 0, b, a)
            w_full[pl.ds((h * 4 + x) * 144, 144), :] = jnp.concatenate([first, second], axis=0).astype(BF)
    for c in copies[2:]:
        c.wait()
    out = jnp.dot(rows[...], w_full[...], preferred_element_type=F32)
    z[...] = out
    n_txt[...] = (out * inverse_length(out)).astype(BF)


def logit_gradient(scal, img_rows, txt_rows):
    logits = scal[0] * lax.dot_general(
        img_rows, txt_rows, (((1,), (1,)), ((), ())), preferred_element_type=F32
    ) + scal[1]
    return 1.0 / (1.0 + jnp.exp(-logits))


def main_kernel(at, scal, n_txt, n_own, n_a, n_b, n_c, z, txt, txt_far, grad, g_own, g_far, mine, other, rows, feat, wide, sems):
    moves = [(block, rows.at[pl.ds(k * 320, 320)]) for k, block in enumerate((n_own, n_a, n_b, n_c))]
    moves += [(txt, feat.at[pl.ds(0, 320)]), (txt_far, feat.at[pl.ds(320, 320)])]
    copies = [pltpu.make_async_copy(a, b, sems.at[k]) for k, (a, b) in enumerate(moves)]
    for c in copies:
        c.start()
    for c in copies[:4]:
        c.wait()
    g = logit_gradient(scal, n_txt[...], rows[...])
    row_ids = lax.broadcasted_iota(jnp.int32, g.shape, 0)
    col_ids = lax.broadcasted_iota(jnp.int32, g.shape, 1)
    grad[...] = (g - jnp.where((row_ids == col_ids) & (row_ids < 320), 1.0, 0.0)).astype(BF)
    total = scal[0] * jnp.dot(grad[...], rows[...], preferred_element_type=F32)
    g_own[...] = total[:320].astype(BF)
    g_far[...] = total[320:].astype(BF)
    for c in copies[4:]:
        c.wait()
    dz = project(total, z[...]).astype(BF)
    wide[...] = lax.dot_general(
        feat[...], dz, (((0,), (0,)), ((), ())), preferred_element_type=F32
    )
    core = at[2]
    for j in range(8):
        a = pl.multiple_of((2 * j + core) * 72, 8)
        b = pl.multiple_of((2 * j + 1 - core) * 72, 8)
        mine[j % 4, j // 4] = wide[pl.ds(a, 72), :].astype(BF)
        other[j % 4, j // 4] = wide[pl.ds(b, 72), :].astype(BF)


def part_kernel(first, scal, grad, n_txt, *outs):
    start = first * 320
    rows = sum(ref.shape[0] for ref in outs)
    out = scal[0] * lax.dot_general(
        grad[:, start : start + rows], n_txt[...], (((0,), (0,)), ((), ())), preferred_element_type=F32
    )
    at = 0
    for ref in outs:
        ref[...] = out[at : at + ref.shape[0]].astype(BF)
        at += ref.shape[0]


def pass_on_kernel(part_a, part_b, got_b, got_a, out_a, out_b):
    out_a[pl.ds(0, 160), :] = part_a[pl.ds(0, 160), :]
    out_a[pl.ds(160, 160), :] = (part_a[pl.ds(160, 160), :].astype(F32) + got_a[...].astype(F32)).astype(BF)
    out_b[pl.ds(0, 160), :] = (part_b[pl.ds(0, 160), :].astype(F32) + got_b[...].astype(F32)).astype(BF)
    out_b[pl.ds(160, 160), :] = part_b[pl.ds(160, 160), :]


def core_sum_kernel(at, mine, got, early, keep, send):
    early[0] = (mine[0, :, :, :EARLY].astype(F32) + got[0, :, :, :EARLY].astype(F32)).astype(BF)
    for out, h in ((keep, at[0]), (send, 1 - at[0])):
        out[0] = (mine[0, h, :, EARLY:].astype(F32) + got[0, h, :, EARLY:].astype(F32)).astype(BF)


def core_sum(at, mine, got):
    late = 1152 - EARLY
    shapes = (2, 72, EARLY), (72, late), (72, late)
    whole = pl.BlockSpec((1, 2, 72, 1152), lambda x: (x, 0, 0, 0))
    return pl.pallas_call(
        core_sum_kernel,
        grid=(4,),
        out_shape=[shaped((4, *s), BF) for s in shapes],
        in_specs=[SM, whole, whole],
        out_specs=[
            pl.BlockSpec((1, *s), lambda x, n=len(s): (x,) + (0,) * n) for s in shapes
        ],
        compiler_params=pltpu.CompilerParams(vmem_limit_bytes=16 * MIB),
        cost_estimate=pl.CostEstimate(flops=1024, bytes_accessed=1024, transcendentals=0),
    )(at, mine, got)


def x_sum_kernel(at, got, keep, send):
    for out, h in ((keep, at[0]), (send, 1 - at[0])):
        a, b, c, d = (got[x, h].astype(F32) for x in range(4))
        out[...] = ((a + b) + (c + d)).astype(BF)


def join_kernel(keep, got, along, out):
    out[:, :EARLY] = (keep[...].astype(F32) + got[...].astype(F32)).astype(BF)
    a, b, c, d = (along[x].astype(F32) for x in range(4))
    out[:, EARLY:] = ((a + b) + (c + d)).astype(BF)


def pair_sum_kernel(a, b, out):
    out[...] = (a[...].astype(F32) + b[...].astype(F32)).astype(BF)


def quad_sum_kernel(a, b, c, d, out):
    total = (a[...].astype(F32) + b[...].astype(F32)) + (c[...].astype(F32) + d[...].astype(F32))
    out[...] = total.astype(out.dtype)


def image_out_kernel(img, a, b, c, out):
    grad = a[...].astype(F32) + (b[...].astype(F32) + c[...].astype(F32))
    out[...] = project(grad, img[...].astype(F32)).astype(BF)


def text_out_kernel(z, a, b, w_full, out, rows, head, sems):
    copies = [
        pltpu.make_async_copy(z.at[pl.ds(0, 320)], rows, sems.at[0]),
        pltpu.make_async_copy(w_full, head, sems.at[1]),
    ]
    for c in copies:
        c.start()
    grad = a[...].astype(F32) + b[...].astype(F32)
    copies[0].wait()
    dz = project(grad, rows[...]).astype(BF)
    copies[1].wait()
    out[...] = lax.dot_general(
        dz, head[...], (((1,), (1,)), ((), ())), preferred_element_type=F32
    ).astype(BF)


def apart(step, *args):
    outs = jax.eval_shape(step, *args)
    return lax.cond(
        lax.axis_index("z") < AXES["z"],
        step,
        lambda *_: tuple(jnp.zeros(o.shape, o.dtype) for o in outs),
        *args,
    )


hold = lax.optimization_barrier
BLOCK = shaped((320, 1152), BF)


def stack_of(*lead):
    return shaped((*lead, 72, 1152), BF)


def along_x(value):
    return lax.all_to_all(value, "x", split_axis=0, concat_axis=0, tiled=True)


def gather_head(at, w_h, w_y):
    (pieces,) = call(repeat_kernel, [stack_of(4, 2)], [SM, VM, VM])(at, w_h, w_y)
    near = along_x(pieces)
    return near, shift(near, "core", 1)


def parts_of(first, shapes, *args):
    kernel = functools.partial(part_kernel, first)
    return call(kernel, shapes, [SM] + [VM] * 2, flops=1 << 31)(*args)


def sum_plane(at, scal, mine, got_core, part_c, grad, n_txt, z, g_own, g_far, w_full):
    early, keep_q, send_q = core_sum(at, mine, got_core)
    early, send_q, part_c = hold((early, send_q, part_c))
    got_x = along_x(early)
    (both_q,) = call(pair_sum_kernel, [shaped(keep_q.shape, BF)], [VM] * 2)(keep_q, swap_far(send_q))
    both_q, grad = hold((both_q, grad))
    along_q = along_x(both_q)
    got_b, got_a = shift(part_c[0], "z", 1), shift(part_c[1], "z", -1)
    part_own, part_a, part_b = parts_of(0, [BLOCK] * 3, scal, grad, n_txt)
    part_a, part_b = call(pass_on_kernel, [BLOCK] * 2, [VM] * 4)(part_a, part_b, got_b, got_a)
    got_a, got_b = shift(part_a, "z", -1), shift(part_b, "z", 1)
    g_got = shift(g_far, "ylo", 1)
    keep, send = call(x_sum_kernel, [shaped((72, EARLY), BF)] * 2, [SM, VM])(at, got_x)
    (one,) = call(join_kernel, [stack_of()], [VM] * 3)(keep, swap_far(send), along_q)
    one, g_got = hold((one, g_got))
    (pair,) = call(pair_sum_kernel, [stack_of()], [VM] * 2)(one, shift(one, "ylo", 1))
    (d_feat,) = call(
        text_out_kernel,
        [BLOCK],
        [ANY, VM, VM, ANY],
        [pltpu.VMEM((320, 1152), F32), pltpu.VMEM((1152, 1152), BF), pltpu.SemaphoreType.DMA((2,))],
        flops=1 << 31,
    )(z, g_own, g_got, w_full)
    pair, d_feat, got_a, got_b = hold((pair, d_feat, got_a, got_b))
    return pair, d_feat, part_own, got_a, got_b


def on_device(img_emb, txt_feat, w_txt, t_log, bias):
    img, txt = img_emb[0], txt_feat[0]
    at = jnp.stack([lax.axis_index(a) for a in ("yhi", "x", "core", "z")]).astype(jnp.int32)
    scal = jnp.concatenate([jnp.exp(t_log), bias])

    txt_far = shift(txt, "ylo", 1)
    (w_h,) = call(half_kernel, [stack_of()], [VM])(w_txt)
    w_y = swap_far(w_h)
    (n_img,) = call(unit_kernel, [BLOCK], [VM, ANY])(img, w_h)
    n_c, n_b, n_a = (shift(n_img, "z", s) for s in (2, -1, 1))
    near, far = apart(gather_head, at, w_h, w_y)
    near, far, txt_far = hold((near, far, txt_far))

    w_full, z, n_txt = call(
        text_kernel,
        [shaped((1152, 1152), BF), shaped((640, 1152), F32), shaped((640, 1152), BF)],
        [SM] + [ANY] * 4,
        [
            pltpu.VMEM((4, 2, 72, 1152), BF),
            pltpu.VMEM((4, 2, 72, 1152), BF),
            pltpu.VMEM((640, 1152), BF),
            pltpu.SemaphoreType.DMA((4,)),
        ],
        vmem=TEXT_MIB,
        flops=1 << 34,
    )(at, near, far, txt, txt_far)
    n_txt, n_a, n_b, n_c = hold((n_txt, n_a, n_b, n_c))
    grad, g_own, g_far, mine, other = call(
        main_kernel,
        [shaped((640, 1280), BF), BLOCK, BLOCK, stack_of(4, 2), stack_of(4, 2)],
        [SM, SM, VM] + [ANY] * 4 + [VM, ANY, ANY],
        [
            pltpu.VMEM((1280, 1152), BF),
            pltpu.VMEM((640, 1152), BF),
            pltpu.VMEM((1152, 1152), F32),
            pltpu.SemaphoreType.DMA((6,)),
        ],
        vmem=MAIN_MIB,
    )(at, scal, n_txt, n_img, n_a, n_b, n_c, z, txt, txt_far)

    half = shaped((160, 1152), BF)
    got_core, part_c = hold(
        (shift(other, "core", 1), parts_of(3, [half] * 2, scal, grad, n_txt))
    )
    quad, d_feat, part_own, got_a, got_b = sum_plane(
        at, scal, mine, got_core, part_c, grad, n_txt, z, g_own, g_far, w_full
    )
    (d_img,) = call(image_out_kernel, [BLOCK], [VM] * 4, flops=1 << 30)(img, part_own, got_a, got_b)
    (d_weight,) = call(quad_sum_kernel, [shaped((72, 1152), F32)], [VM] * 4)(
        quad, shift(quad, "z", 2), shift(quad, "z", 1), shift(quad, "z", -1)
    )
    return (d_img[None], d_feat[None], d_weight)


def solution(mesh):
    fine = Mesh(mesh.devices.reshape(2, 4, 2, 4, 2), tuple(AXES))
    dp, fsdp = ("ylo", "z"), ("yhi", "x", "core")
    placed = (P(fsdp, dp, None), P(fsdp, dp, None), P(fsdp, None), P(), P())
    return jax.shard_map(
        on_device,
        mesh=fine,
        in_specs=placed,
        out_specs=(P(fsdp, dp, None), P(fsdp, dp, None), P(fsdp, None)),
        check_vma=False,
    )
```

```python
import functools

import jax
import jax.numpy as jnp
from jax import lax
from jax.experimental import pallas as pl
from jax.experimental.pallas import tpu as pltpu
from jax.sharding import Mesh, PartitionSpec as P

BF = jnp.bfloat16
F32 = jnp.float32
MIB = 1024 * 1024
TEXT_MIB = 14
MAIN_MIB = 24
AXES = {"ylo": 2, "z": 4, "yhi": 2, "x": 4, "core": 2}

VM = pl.BlockSpec(memory_space=pltpu.VMEM)
SM = pl.BlockSpec(memory_space=pltpu.SMEM)
ANY = pl.BlockSpec(memory_space=pl.ANY)


def shift(value, axis, step):
    n = AXES[axis]
    return lax.ppermute(value, axis, [(i, (i + step) % n) for i in range(n)])


def apart_by_core(value):
    pairs = [(z * 2 + c, (z + 1 - 2 * c) % 4 * 2 + c) for z in range(4) for c in range(2)]
    return lax.ppermute(value, ("z", "core"), pairs)


def swap_far(value):
    pairs = [(a * 2 + b, (1 - a) * 2 + 1 - b) for a in range(2) for b in range(2)]
    return lax.ppermute(value, ("ylo", "yhi"), pairs)


def shaped(shape, dtype):
    return jax.ShapeDtypeStruct(shape, dtype)


def call(kernel, outs, specs, scratch=(), vmem=10, out_specs=None, flops=1024):
    return pl.pallas_call(
        kernel,
        out_shape=outs,
        in_specs=specs,
        out_specs=out_specs or [VM] * len(outs),
        scratch_shapes=list(scratch),
        compiler_params=pltpu.CompilerParams(vmem_limit_bytes=vmem * MIB),
        cost_estimate=pl.CostEstimate(flops=flops, bytes_accessed=1024, transcendentals=0),
    )


def inverse_length(rows):
    return 1.0 / jnp.sqrt(jnp.sum(rows * rows, axis=-1, keepdims=True) + 1e-06)


def project(grad, rows):
    inv = inverse_length(rows)
    unit = rows * inv
    inner = jnp.sum(unit * grad, axis=-1, keepdims=True)
    return (grad - unit * inner) * inv


def half_kernel(w, w_half):
    w_half[...] = w[...].astype(BF)


def repeat_kernel(w_h, w_y, out):
    yhi = lax.axis_index("yhi")
    for k in range(4):
        out[k, yhi] = w_h[...]
        out[k, 1 - yhi] = w_y[...]


def unit_kernel(img, _, n_img):
    rows = img[...].astype(F32)
    n_img[...] = (rows * inverse_length(rows)).astype(BF)


def assemble(mine, other, head):
    core = lax.axis_index("core")
    for x in range(4):
        for h in range(2):
            a, b = mine[x, h].astype(F32), other[x, h].astype(F32)
            first = jnp.where(core == 0, a, b)
            second = jnp.where(core == 0, b, a)
            head[pl.ds((h * 4 + x) * 144, 144), :] = jnp.concatenate([first, second], axis=0).astype(BF)


def text_kernel(near, far, txt, txt_far, z, n_txt, mine, other, rows, w_full, sems):
    copies = [
        pltpu.make_async_copy(near, mine, sems.at[0]),
        pltpu.make_async_copy(far, other, sems.at[1]),
        pltpu.make_async_copy(txt, rows.at[pl.ds(0, 320)], sems.at[2]),
        pltpu.make_async_copy(txt_far, rows.at[pl.ds(320, 320)], sems.at[3]),
    ]
    for c in copies:
        c.start()
    for c in copies[:2]:
        c.wait()
    assemble(mine, other, w_full)
    for c in copies[2:]:
        c.wait()
    out = jnp.dot(rows[...], w_full[...], preferred_element_type=F32)
    z[...] = out
    n_txt[...] = (out * inverse_length(out)).astype(BF)


def scale_of(t_log):
    return jnp.exp(jnp.full((1, 1), t_log[0], F32))


def logit_gradient(scale, bias, left, right):
    logits = scale * lax.dot_general(
        left, right, (((1,), (1,)), ((), ())), preferred_element_type=F32
    ) + bias[0]
    return 1.0 / (1.0 + jnp.exp(-logits))


def main_kernel(t_log, bias, n_txt, n_own, n_a, n_b, n_c, z, txt, txt_far, grad, g_own, g_far, mine, other, rows, feat, wide, sems):
    moves = [(block, rows.at[pl.ds(k * 320, 320)]) for k, block in enumerate((n_own, n_a, n_b, n_c))]
    moves += [(txt, feat.at[pl.ds(0, 320)]), (txt_far, feat.at[pl.ds(320, 320)])]
    copies = [pltpu.make_async_copy(a, b, sems.at[k]) for k, (a, b) in enumerate(moves)]
    for c in copies:
        c.start()
    for c in copies[:4]:
        c.wait()
    scale = scale_of(t_log)
    g = logit_gradient(scale, bias, n_txt[...], rows[...])
    row_ids = lax.broadcasted_iota(jnp.int32, g.shape, 0)
    col_ids = lax.broadcasted_iota(jnp.int32, g.shape, 1)
    grad[...] = (g - jnp.where((row_ids == col_ids) & (row_ids < 320), 1.0, 0.0)).astype(BF)
    total = scale * jnp.dot(grad[...], rows[...], preferred_element_type=F32)
    g_own[...] = total[:320].astype(BF)
    g_far[...] = total[320:].astype(BF)
    for c in copies[4:]:
        c.wait()
    dz = project(total, z[...]).astype(BF)
    wide[...] = lax.dot_general(
        feat[...], dz, (((0,), (0,)), ((), ())), preferred_element_type=F32
    )
    core = lax.axis_index("core")
    for j in range(8):
        a = pl.multiple_of((2 * j + core) * 72, 8)
        b = pl.multiple_of((2 * j + 1 - core) * 72, 8)
        mine[j % 4, j // 4] = wide[pl.ds(a, 72), :].astype(BF)
        other[j % 4, j // 4] = wide[pl.ds(b, 72), :].astype(BF)


def part_kernel(first, t_log, grad, n_txt, *outs):
    start = first * 320
    rows = sum(ref.shape[0] for ref in outs)
    out = scale_of(t_log) * lax.dot_general(
        grad[:, start : start + rows], n_txt[...], (((0,), (0,)), ((), ())), preferred_element_type=F32
    )
    at = 0
    for ref in outs:
        ref[...] = out[at : at + ref.shape[0]].astype(BF)
        at += ref.shape[0]


def pass_on_kernel(part_a, part_b, got, out_a, out_b):
    first = lax.axis_index("core") == 0
    for part, out, take in ((part_a, out_a, jnp.logical_not(first)), (part_b, out_b, first)):
        out[...] = (part[...].astype(F32) + jnp.where(take, got[...].astype(F32), 0.0)).astype(BF)


def core_sum_kernel(mine, got, *outs):
    x = lax.axis_index("x")
    for r, out in enumerate(outs):
        k = (x + r) % 4
        out[...] = (mine[k].astype(F32) + got[k].astype(F32)).astype(BF)


def x_sum_kernel(own, p, q, r, keep, send):
    yhi = lax.axis_index("yhi")
    for out, h in ((keep, yhi), (send, 1 - yhi)):
        a, b, c, d = (part[h].astype(F32) for part in (own, p, q, r))
        out[...] = ((a + b) + (c + d)).astype(BF)


def pair_sum_kernel(a, b, out):
    out[...] = (a[...].astype(F32) + b[...].astype(F32)).astype(BF)


def quad_sum_kernel(a, b, c, d, out):
    total = (a[...].astype(F32) + b[...].astype(F32)) + (c[...].astype(F32) + d[...].astype(F32))
    out[...] = total.astype(out.dtype)


def image_out_kernel(img, a, b, c, out):
    grad = a[...].astype(F32) + (b[...].astype(F32) + c[...].astype(F32))
    out[...] = project(grad, img[...].astype(F32)).astype(BF)


def text_out_kernel(z, a, b, near, far, out, rows, mine, other, head, sems):
    moves = (near, mine), (far, other), (z.at[pl.ds(0, 320)], rows)
    copies = [pltpu.make_async_copy(x, y, sems.at[k]) for k, (x, y) in enumerate(moves)]
    for c in copies:
        c.start()
    for c in copies:
        c.wait()
    assemble(mine, other, head)
    dz = project(a[...].astype(F32) + b[...].astype(F32), rows[...]).astype(BF)
    out[...] = lax.dot_general(
        dz, head[...], (((1,), (1,)), ((), ())), preferred_element_type=F32
    ).astype(BF)


def apart(step, *args):
    outs = jax.eval_shape(step, *args)
    return lax.cond(
        lax.axis_index("z") < AXES["z"],
        step,
        lambda *_: jax.tree.map(lambda o: jnp.zeros(o.shape, o.dtype), outs),
        *args,
    )


hold = lax.optimization_barrier
BLOCK = shaped((320, 1152), BF)


def stack_of(*lead):
    return shaped((*lead, 72, 1152), BF)


def along_x(value):
    return lax.all_to_all(value, "x", split_axis=0, concat_axis=0, tiled=True)


def gather_head(w_h, w_y):
    (pieces,) = call(repeat_kernel, [stack_of(4, 2)], [VM, VM])(w_h, w_y)
    near = along_x(pieces)
    return near, shift(near, "core", 1)


def parts_of(first, shapes, *args):
    kernel = functools.partial(part_kernel, first)
    return call(kernel, shapes, [SM] + [VM] * 2, flops=1 << 31)(*args)


def beside_x(part_c, t_log, grad, n_txt):
    got_c = apart_by_core(part_c)
    part_own, part_a, part_b = parts_of(0, [BLOCK] * 3, t_log, grad, n_txt)
    return part_own, *call(pass_on_kernel, [BLOCK] * 2, [VM] * 3)(part_a, part_b, got_c)


def sum_plane(t_log, mine, got_core, part_c, grad, n_txt, z, g_own, g_far, near, far):
    rel = call(core_sum_kernel, [stack_of(2)] * 4, [VM] * 2)(mine, got_core)
    got_x = [shift(rel[s], "x", s) for s in (1, 3, 2)]
    g_got = shift(g_far, "ylo", 1)
    part_own, part_a, part_b = beside_x(part_c, t_log, grad, n_txt)
    got_x[2], part_a, part_b = hold((got_x[2], part_a, part_b))
    keep, send = call(x_sum_kernel, [stack_of()] * 2, [VM] * 4)(rel[0], *got_x)
    got_a, got_b = shift(part_a, "z", -1), shift(part_b, "z", 1)
    (d_feat,) = call(
        text_out_kernel,
        [BLOCK],
        [ANY, VM, VM, ANY, ANY],
        [
            pltpu.VMEM((320, 1152), F32),
            pltpu.VMEM((4, 2, 72, 1152), BF),
            pltpu.VMEM((4, 2, 72, 1152), BF),
            pltpu.VMEM((1152, 1152), BF),
            pltpu.SemaphoreType.DMA((3,)),
        ],
        vmem=50,
        flops=1 << 31,
    )(z, g_own, g_got, near, far)
    (one,) = call(pair_sum_kernel, [stack_of()], [VM] * 2)(keep, swap_far(send))
    (pair,) = call(pair_sum_kernel, [stack_of()], [VM] * 2)(one, shift(one, "ylo", 1))
    pair, d_feat = hold((pair, d_feat))
    return pair, d_feat, part_own, got_a, got_b


def on_device(img_emb, txt_feat, w_txt, t_log, bias):
    img, txt = img_emb[0], txt_feat[0]

    txt_far = shift(txt, "ylo", 1)
    (w_h,) = call(half_kernel, [stack_of()], [VM])(w_txt)
    w_y = swap_far(w_h)
    (n_img,) = call(unit_kernel, [BLOCK], [VM, ANY])(img, w_h)
    n_c, n_b, n_a = (shift(n_img, "z", s) for s in (2, -1, 1))
    near, far = apart(gather_head, w_h, w_y)
    near, far, txt_far = hold((near, far, txt_far))

    z, n_txt = call(
        text_kernel,
        [shaped((640, 1152), F32), shaped((640, 1152), BF)],
        [ANY] * 4,
        [
            pltpu.VMEM((4, 2, 72, 1152), BF),
            pltpu.VMEM((4, 2, 72, 1152), BF),
            pltpu.VMEM((640, 1152), BF),
            pltpu.VMEM((1152, 1152), BF),
            pltpu.SemaphoreType.DMA((4,)),
        ],
        vmem=TEXT_MIB,
        flops=1 << 34,
    )(near, far, txt, txt_far)
    n_txt, n_a, n_b, n_c = hold((n_txt, n_a, n_b, n_c))
    grad, g_own, g_far, mine, other = call(
        main_kernel,
        [shaped((640, 1280), BF), BLOCK, BLOCK, stack_of(4, 2), stack_of(4, 2)],
        [SM, SM, VM] + [ANY] * 4 + [VM, ANY, ANY],
        [
            pltpu.VMEM((1280, 1152), BF),
            pltpu.VMEM((640, 1152), BF),
            pltpu.VMEM((1152, 1152), F32),
            pltpu.SemaphoreType.DMA((6,)),
        ],
        vmem=MAIN_MIB,
    )(t_log, bias, n_txt, n_img, n_a, n_b, n_c, z, txt, txt_far)

    got_core, (part_c,) = hold(
        (shift(other, "core", 1), parts_of(3, [BLOCK], t_log, grad, n_txt))
    )
    quad, d_feat, part_own, got_a, got_b = sum_plane(
        t_log, mine, got_core, part_c, grad, n_txt, z, g_own, g_far, near, far
    )
    (d_img,) = call(image_out_kernel, [BLOCK], [VM] * 4, flops=1 << 30)(img, part_own, got_a, got_b)
    got_z = [shift(quad, "z", k) for k in (2, 1, -1)]
    got_z, d_img = hold((got_z, d_img))
    (d_weight,) = call(quad_sum_kernel, [shaped((72, 1152), F32)], [VM] * 4)(quad, *got_z)
    return (d_img[None], d_feat[None], d_weight)


def solution(mesh):
    fine = Mesh(mesh.devices.reshape(2, 4, 2, 4, 2), tuple(AXES))
    dp, fsdp = ("ylo", "z"), ("yhi", "x", "core")
    placed = (P(fsdp, dp, None), P(fsdp, dp, None), P(fsdp, None), P(), P())
    return jax.shard_map(
        on_device,
        mesh=fine,
        in_specs=placed,
        out_specs=(P(fsdp, dp, None), P(fsdp, dp, None), P(fsdp, None)),
        check_vma=False,
    )
```

```python
import functools

import jax
import jax.numpy as jnp
from jax import lax
from jax.experimental import pallas as pl
from jax.experimental.pallas import tpu as pltpu
from jax.sharding import Mesh, PartitionSpec as P

BF = jnp.bfloat16
F32 = jnp.float32
MIB = 1024 * 1024
TEXT_MIB = 14
MAIN_MIB = 28
AXES = {"ylo": 2, "z": 4, "yhi": 2, "x": 4, "core": 2}

VM = pl.BlockSpec(memory_space=pltpu.VMEM)
SM = pl.BlockSpec(memory_space=pltpu.SMEM)
ANY = pl.BlockSpec(memory_space=pl.ANY)


def shift(value, axis, step):
    n = AXES[axis]
    return lax.ppermute(value, axis, [(i, (i + step) % n) for i in range(n)])


def apart_by_core(value):
    pairs = [(z * 2 + c, (z + 1 - 2 * c) % 4 * 2 + c) for z in range(4) for c in range(2)]
    return lax.ppermute(value, ("z", "core"), pairs)


def swap_far(value):
    pairs = [(a * 2 + b, (1 - a) * 2 + 1 - b) for a in range(2) for b in range(2)]
    return lax.ppermute(value, ("ylo", "yhi"), pairs)


def shaped(shape, dtype):
    return jax.ShapeDtypeStruct(shape, dtype)


def call(kernel, outs, specs, scratch=(), vmem=10, out_specs=None, flops=1024):
    return pl.pallas_call(
        kernel,
        out_shape=outs,
        in_specs=specs,
        out_specs=out_specs or [VM] * len(outs),
        scratch_shapes=list(scratch),
        compiler_params=pltpu.CompilerParams(vmem_limit_bytes=vmem * MIB),
        cost_estimate=pl.CostEstimate(flops=flops, bytes_accessed=1024, transcendentals=0),
    )


def inverse_length(rows):
    return 1.0 / jnp.sqrt(jnp.sum(rows * rows, axis=-1, keepdims=True) + 1e-06)


def project(grad, rows):
    inv = inverse_length(rows)
    unit = rows * inv
    inner = jnp.sum(unit * grad, axis=-1, keepdims=True)
    return (grad - unit * inner) * inv


def half_kernel(w, w_half):
    w_half[...] = w[...].astype(BF)


def repeat_kernel(w_h, w_y, out):
    yhi = lax.axis_index("yhi")
    for k in range(4):
        out[k, yhi] = w_h[...]
        out[k, 1 - yhi] = w_y[...]


def load_head(near, far, mine, other, sems):
    copies = [
        pltpu.make_async_copy(src.at[x], dst.at[x], sems.at[2 * x + k])
        for x in range(4)
        for k, (src, dst) in enumerate(((near, mine), (far, other)))
    ]
    for c in copies:
        c.start()
    return copies


def assemble(copies, mine, other, head):
    core = lax.axis_index("core")
    for x in range(4):
        copies[2 * x].wait()
        copies[2 * x + 1].wait()
        for h in range(2):
            a, b = mine[x, h].astype(F32), other[x, h].astype(F32)
            first = jnp.where(core == 0, a, b)
            second = jnp.where(core == 0, b, a)
            head[pl.ds((h * 4 + x) * 144, 144), :] = jnp.concatenate([first, second], axis=0).astype(BF)


def text_kernel(near, far, txt, txt_far, z, n_txt, mine, other, rows, w_full, sems):
    copies = load_head(near, far, mine, other, sems)
    late = [
        pltpu.make_async_copy(txt, rows.at[pl.ds(0, 320)], sems.at[8]),
        pltpu.make_async_copy(txt_far, rows.at[pl.ds(320, 320)], sems.at[9]),
    ]
    for c in late:
        c.start()
    assemble(copies, mine, other, w_full)
    for c in late:
        c.wait()
    out = jnp.dot(rows[...], w_full[...], preferred_element_type=F32)
    z[...] = out
    n_txt[...] = (out * inverse_length(out)).astype(BF)


def logit_gradient(scale, bias, left, right):
    logits = scale * lax.dot_general(
        left, right, (((1,), (1,)), ((), ())), preferred_element_type=F32
    ) + bias
    return 1.0 / (1.0 + jnp.exp(-logits))


def main_kernel(t_log, bias, n_txt, img, img_a, img_b, img_c, z, txt, txt_far, grad, g_own, g_far, mine, other, raw, rows, feat, wide, sems):
    moves = [(block, raw.at[pl.ds(k * 320, 320)]) for k, block in enumerate((img, img_a, img_b, img_c))]
    moves += [(txt, feat.at[pl.ds(0, 320)]), (txt_far, feat.at[pl.ds(320, 320)])]
    copies = [pltpu.make_async_copy(a, b, sems.at[k]) for k, (a, b) in enumerate(moves)]
    for c in copies:
        c.start()
    scale = jnp.exp(t_log[...])
    for first, last, ready in ((0, 512, copies[:2]), (512, 1280, copies[2:4])):
        for c in ready:
            c.wait()
        fresh = pl.ds(0 if first == 0 else 640, 640)
        wide_rows = raw[fresh, :].astype(F32)
        rows[fresh, :] = (wide_rows * inverse_length(wide_rows)).astype(BF)
        g = logit_gradient(scale, bias[...], n_txt[...], rows[pl.ds(first, last - first), :])
        row_ids = lax.broadcasted_iota(jnp.int32, g.shape, 0)
        col_ids = lax.broadcasted_iota(jnp.int32, g.shape, 1)
        if first == 0:
            g = g - jnp.where((row_ids == col_ids) & (row_ids < 320), 1.0, 0.0)
        grad[:, first:last] = g.astype(BF)
    total = scale * jnp.dot(grad[...], rows[...], preferred_element_type=F32)
    g_own[...] = total[:320].astype(BF)
    g_far[...] = total[320:].astype(BF)
    for c in copies[4:]:
        c.wait()
    dz = project(total, z[...]).astype(BF)
    wide[...] = lax.dot_general(
        feat[...], dz, (((0,), (0,)), ((), ())), preferred_element_type=F32
    )
    core = lax.axis_index("core")
    for j in range(8):
        a = pl.multiple_of((2 * j + core) * 72, 8)
        b = pl.multiple_of((2 * j + 1 - core) * 72, 8)
        mine[j % 4, j // 4] = wide[pl.ds(a, 72), :].astype(BF)
        other[j % 4, j // 4] = wide[pl.ds(b, 72), :].astype(BF)


def part_kernel(first, t_log, grad, n_txt, *outs):
    start = first * 320
    rows = sum(ref.shape[0] for ref in outs)
    out = jnp.exp(t_log[...]) * lax.dot_general(
        grad[:, start : start + rows], n_txt[...], (((0,), (0,)), ((), ())), preferred_element_type=F32
    )
    at = 0
    for ref in outs:
        ref[...] = out[at : at + ref.shape[0]].astype(BF)
        at += ref.shape[0]


def pass_on_kernel(part_a, part_b, got, out_a, out_b):
    first = lax.axis_index("core") == 0
    for part, out, take in ((part_a, out_a, jnp.logical_not(first)), (part_b, out_b, first)):
        out[...] = (part[...].astype(F32) + jnp.where(take, got[...].astype(F32), 0.0)).astype(BF)


def core_sum_kernel(mine, got, *outs):
    x = lax.axis_index("x")
    for r, out in enumerate(outs):
        k = (x + r) % 4
        out[...] = (mine[k].astype(F32) + got[k].astype(F32)).astype(BF)


def x_sum_kernel(own, p, q, r, keep, send):
    yhi = lax.axis_index("yhi")
    for out, h in ((keep, yhi), (send, 1 - yhi)):
        a, b, c, d = (part[h].astype(F32) for part in (own, p, q, r))
        out[...] = ((a + b) + (c + d)).astype(BF)


def pair_sum_kernel(a, b, out):
    out[...] = (a[...].astype(F32) + b[...].astype(F32)).astype(BF)


def quad_sum_kernel(a, b, c, d, out):
    total = (a[...].astype(F32) + b[...].astype(F32)) + (c[...].astype(F32) + d[...].astype(F32))
    out[...] = total.astype(out.dtype)


def image_out_kernel(img, a, b, c, out):
    grad = a[...].astype(F32) + (b[...].astype(F32) + c[...].astype(F32))
    out[...] = project(grad, img[...].astype(F32)).astype(BF)


def head_kernel(near, far, head, mine, other, sems):
    assemble(load_head(near, far, mine, other, sems), mine, other, head)


def text_out_kernel(z, a, b, head, out, rows, sems):
    copy = pltpu.make_async_copy(z.at[pl.ds(0, 320)], rows, sems.at[0])
    copy.start()
    grad = a[...].astype(F32) + b[...].astype(F32)
    copy.wait()
    dz = project(grad, rows[...]).astype(BF)
    out[...] = lax.dot_general(
        dz, head[...], (((1,), (1,)), ((), ())), preferred_element_type=F32
    ).astype(BF)


def apart(step, *args):
    outs = jax.eval_shape(step, *args)
    return lax.cond(
        lax.axis_index("z") < AXES["z"],
        step,
        lambda *_: jax.tree.map(lambda o: jnp.zeros(o.shape, o.dtype), outs),
        *args,
    )


hold = lax.optimization_barrier
BLOCK = shaped((320, 1152), BF)


def stack_of(*lead):
    return shaped((*lead, 72, 1152), BF)


def along_x(value):
    return lax.all_to_all(value, "x", split_axis=0, concat_axis=0, tiled=True)


def gather_head(w_h, w_y):
    (pieces,) = call(repeat_kernel, [stack_of(4, 2)], [VM, VM])(w_h, w_y)
    near = along_x(pieces)
    return near, shift(near, "core", 1)


def parts_of(first, shapes, *args):
    kernel = functools.partial(part_kernel, first)
    return call(kernel, shapes, [VM] * 3, flops=1 << 31)(*args)


def beside_x(part_c, t_log, grad, n_txt):
    got_c = apart_by_core(part_c)
    part_own, part_a, part_b = parts_of(0, [BLOCK] * 3, t_log, grad, n_txt)
    return part_own, *call(pass_on_kernel, [BLOCK] * 2, [VM] * 3)(part_a, part_b, got_c)


def sum_plane(t_log, mine, got_core, part_c, grad, n_txt, z, g_own, g_far, near, far):
    rel = call(core_sum_kernel, [stack_of(2)] * 4, [VM] * 2)(mine, got_core)
    got_x = [shift(rel[s], "x", s) for s in (1, 3, 2)]
    g_got = shift(g_far, "ylo", 1)
    part_own, part_a, part_b = beside_x(part_c, t_log, grad, n_txt)
    got_x[2], part_a, part_b, near, far = hold((got_x[2], part_a, part_b, near, far))
    (head,) = call(
        head_kernel,
        [shaped((1152, 1152), BF)],
        [ANY] * 2,
        [
            pltpu.VMEM((4, 2, 72, 1152), BF),
            pltpu.VMEM((4, 2, 72, 1152), BF),
            pltpu.SemaphoreType.DMA((8,)),
        ],
        flops=1 << 31,
    )(near, far)
    got_x[:2], head = hold((got_x[:2], head))
    keep, send = call(x_sum_kernel, [stack_of()] * 2, [VM] * 4)(rel[0], *got_x)
    got_a, got_b = shift(part_a, "z", -1), shift(part_b, "z", 1)
    (d_feat,) = call(
        text_out_kernel,
        [BLOCK],
        [ANY, VM, VM, VM],
        [pltpu.VMEM((320, 1152), F32), pltpu.SemaphoreType.DMA((1,))],
        flops=1 << 31,
    )(z, g_own, g_got, head)
    (one,) = call(pair_sum_kernel, [stack_of()], [VM] * 2)(keep, swap_far(send))
    (pair,) = call(pair_sum_kernel, [stack_of()], [VM] * 2)(one, shift(one, "ylo", 1))
    pair, d_feat = hold((pair, d_feat))
    return pair, d_feat, part_own, got_a, got_b


def on_device(img_emb, txt_feat, w_txt, t_log, bias):
    img, txt = img_emb[0], txt_feat[0]
    t_log, bias = t_log.reshape(1, 1), bias.reshape(1, 1)

    txt_far = shift(txt, "ylo", 1)
    (w_h,) = call(half_kernel, [stack_of()], [VM], vmem=60)(w_txt)
    w_y = swap_far(w_h)
    w_h, img = hold((w_h, img))
    img_c, img_b, img_a = (shift(img, "z", s) for s in (2, -1, 1))
    near, far = apart(gather_head, w_h, w_y)
    near, far, txt_far = hold((near, far, txt_far))

    z, n_txt = call(
        text_kernel,
        [shaped((640, 1152), F32), shaped((640, 1152), BF)],
        [ANY] * 4,
        [
            pltpu.VMEM((4, 2, 72, 1152), BF),
            pltpu.VMEM((4, 2, 72, 1152), BF),
            pltpu.VMEM((640, 1152), BF),
            pltpu.VMEM((1152, 1152), BF),
            pltpu.SemaphoreType.DMA((10,)),
        ],
        vmem=TEXT_MIB,
        flops=1 << 34,
    )(near, far, txt, txt_far)
    n_txt, img_a, img_b, img_c = hold((n_txt, img_a, img_b, img_c))
    grad, g_own, g_far, mine, other = call(
        main_kernel,
        [shaped((640, 1280), BF), BLOCK, BLOCK, stack_of(4, 2), stack_of(4, 2)],
        [VM] * 3 + [ANY] * 4 + [VM, ANY, ANY],
        [
            pltpu.VMEM((1280, 1152), BF),
            pltpu.VMEM((1280, 1152), BF),
            pltpu.VMEM((640, 1152), BF),
            pltpu.VMEM((1152, 1152), F32),
            pltpu.SemaphoreType.DMA((6,)),
        ],
        vmem=MAIN_MIB,
    )(t_log, bias, n_txt, img, img_a, img_b, img_c, z, txt, txt_far)

    got_core, (part_c,) = hold(
        (shift(other, "core", 1), parts_of(3, [BLOCK], t_log, grad, n_txt))
    )
    quad, d_feat, part_own, got_a, got_b = sum_plane(
        t_log, mine, got_core, part_c, grad, n_txt, z, g_own, g_far, near, far
    )
    (d_img,) = call(image_out_kernel, [BLOCK], [VM] * 4, flops=1 << 30)(img, part_own, got_a, got_b)
    got_z = [shift(quad, "z", k) for k in (2, 1, -1)]
    got_z, d_img = hold((got_z, d_img))
    (d_weight,) = call(quad_sum_kernel, [shaped((72, 1152), F32)], [VM] * 4)(quad, *got_z)
    return (d_img[None], d_feat[None], d_weight)


def solution(mesh):
    fine = Mesh(mesh.devices.reshape(2, 4, 2, 4, 2), tuple(AXES))
    dp, fsdp = ("ylo", "z"), ("yhi", "x", "core")
    placed = (P(fsdp, dp, None), P(fsdp, dp, None), P(fsdp, None), P(), P())
    return jax.shard_map(
        on_device,
        mesh=fine,
        in_specs=placed,
        out_specs=(P(fsdp, dp, None), P(fsdp, dp, None), P(fsdp, None)),
        check_vma=False,
    )
```

```python
import functools

import jax
import jax.numpy as jnp
from jax import lax
from jax.experimental import pallas as pl
from jax.experimental.pallas import tpu as pltpu
from jax.sharding import Mesh, PartitionSpec as P

BF = jnp.bfloat16
F32 = jnp.float32
MIB = 1024 * 1024
TEXT_MIB = 14
MAIN_MIB = 28
AXES = {"ylo": 2, "z": 4, "yhi": 2, "x": 4, "core": 2}

VM = pl.BlockSpec(memory_space=pltpu.VMEM)
SM = pl.BlockSpec(memory_space=pltpu.SMEM)
ANY = pl.BlockSpec(memory_space=pl.ANY)


def shift(value, axis, step):
    n = AXES[axis]
    return lax.ppermute(value, axis, [(i, (i + step) % n) for i in range(n)])


def apart_by_core(value):
    pairs = [(z * 2 + c, (z + 1 - 2 * c) % 4 * 2 + c) for z in range(4) for c in range(2)]
    return lax.ppermute(value, ("z", "core"), pairs)


def swap_far(value):
    pairs = [(a * 2 + b, (1 - a) * 2 + 1 - b) for a in range(2) for b in range(2)]
    return lax.ppermute(value, ("ylo", "yhi"), pairs)


def shaped(shape, dtype):
    return jax.ShapeDtypeStruct(shape, dtype)


def call(kernel, outs, specs, scratch=(), vmem=10, out_specs=None, flops=1024):
    return pl.pallas_call(
        kernel,
        out_shape=outs,
        in_specs=specs,
        out_specs=out_specs or [VM] * len(outs),
        scratch_shapes=list(scratch),
        compiler_params=pltpu.CompilerParams(vmem_limit_bytes=vmem * MIB),
        cost_estimate=pl.CostEstimate(flops=flops, bytes_accessed=1024, transcendentals=0),
    )


def inverse_length(rows):
    return 1.0 / jnp.sqrt(jnp.sum(rows * rows, axis=-1, keepdims=True) + 1e-06)


def project(grad, rows, inv=None, scale=1.0):
    inv = inverse_length(rows) if inv is None else inv
    inner = jnp.sum(rows * grad, axis=-1, keepdims=True)
    return (grad - rows * (inv * inv * inner)) * (inv * scale)


def half_kernel(w, w_half):
    w_half[...] = w[...].astype(BF)


def scalar_kernel(t_log, bias, out):
    row_ids = lax.broadcasted_iota(jnp.int32, out.shape, 0)
    out[...] = jnp.where(row_ids == 0, jnp.exp(t_log[...]), bias[...])


def repeat_kernel(w_h, w_y, out):
    yhi = lax.axis_index("yhi")
    for k in range(4):
        out[k, yhi] = w_h[...]
        out[k, 1 - yhi] = w_y[...]


def load_head(near, far, mine, other, sems):
    copies = [
        pltpu.make_async_copy(src.at[x], dst.at[x], sems.at[2 * x + k])
        for x in range(4)
        for k, (src, dst) in enumerate(((near, mine), (far, other)))
    ]
    for c in copies:
        c.start()
    return copies


def assemble(copies, mine, other, head):
    core = lax.axis_index("core")
    for x in range(4):
        copies[2 * x].wait()
        copies[2 * x + 1].wait()
        for h in range(2):
            a, b = mine[x, h].astype(F32), other[x, h].astype(F32)
            first = jnp.where(core == 0, a, b)
            second = jnp.where(core == 0, b, a)
            head[pl.ds((h * 4 + x) * 144, 144), :] = jnp.concatenate([first, second], axis=0).astype(BF)


def text_kernel(near, far, txt, txt_far, z, n_txt, inv, mine, other, rows, w_full, sems):
    copies = load_head(near, far, mine, other, sems)
    late = [
        pltpu.make_async_copy(txt, rows.at[pl.ds(0, 320)], sems.at[8]),
        pltpu.make_async_copy(txt_far, rows.at[pl.ds(320, 320)], sems.at[9]),
    ]
    for c in late:
        c.start()
    assemble(copies, mine, other, w_full)
    for c in late:
        c.wait()
    out = jnp.dot(rows[...], w_full[...], preferred_element_type=F32)
    z[...] = out
    inv[...] = inverse_length(out)
    n_txt[...] = (out * inv[...]).astype(BF)


def logit_gradient(scale, bias, left, right):
    logits = scale * lax.dot_general(
        left, right, (((1,), (1,)), ((), ())), preferred_element_type=F32
    ) + bias
    return 1.0 / (1.0 + jnp.exp(-logits))


def main_kernel(scalars, n_txt, img, img_a, img_b, img_c, z, inv, txt, txt_far, grad, g_own, g_far, mine, other, raw, rows, feat, wide, sems):
    moves = [(block, raw.at[pl.ds(k * 320, 320)]) for k, block in enumerate((img, img_a, img_b, img_c))]
    moves += [(txt, feat.at[pl.ds(0, 320)]), (txt_far, feat.at[pl.ds(320, 320)])]
    copies = [pltpu.make_async_copy(a, b, sems.at[k]) for k, (a, b) in enumerate(moves)]
    for c in copies:
        c.start()
    scale, bias = scalars[0:1, 0:1], scalars[1:2, 0:1]
    for first, last, ready in ((0, 512, copies[:2]), (512, 1280, copies[2:4])):
        for c in ready:
            c.wait()
        fresh = pl.ds(0 if first == 0 else 640, 640)
        wide_rows = raw[fresh, :].astype(F32)
        rows[fresh, :] = (wide_rows * inverse_length(wide_rows)).astype(BF)
        g = logit_gradient(scale, bias, n_txt[...], rows[pl.ds(first, last - first), :])
        grad[:, first:last] = g.astype(BF)
        if first == 0:
            own = g[:320, :384]
            row_ids = lax.broadcasted_iota(jnp.int32, own.shape, 0)
            col_ids = lax.broadcasted_iota(jnp.int32, own.shape, 1)
            grad[:320, :384] = (own - jnp.where(row_ids == col_ids, 1.0, 0.0)).astype(BF)
    parts = []
    for half, out in enumerate((g_own, g_far)):
        here = pl.ds(half * 320, 320)
        total = jnp.dot(grad[here, :], rows[...], preferred_element_type=F32)
        out[...] = (scale * total).astype(BF)
        parts.append(project(total, z[here, :], inv[here, :], scale).astype(BF))
    dz = jnp.concatenate(parts, axis=0)
    for c in copies[4:]:
        c.wait()
    wide[...] = lax.dot_general(
        feat[...], dz, (((0,), (0,)), ((), ())), preferred_element_type=F32
    )
    core = lax.axis_index("core")
    for j in range(8):
        a = pl.multiple_of((2 * j + core) * 72, 8)
        b = pl.multiple_of((2 * j + 1 - core) * 72, 8)
        mine[j % 4, j // 4] = wide[pl.ds(a, 72), :].astype(BF)
        other[j % 4, j // 4] = wide[pl.ds(b, 72), :].astype(BF)


def part_kernel(first, scalars, grad, n_txt, *outs):
    start = first * 320
    rows = sum(ref.shape[0] for ref in outs)
    out = scalars[0:1, 0:1] * lax.dot_general(
        grad[:, start : start + rows], n_txt[...], (((0,), (0,)), ((), ())), preferred_element_type=F32
    )
    at = 0
    for ref in outs:
        ref[...] = out[at : at + ref.shape[0]].astype(BF)
        at += ref.shape[0]


def pass_on_kernel(part_a, part_b, got, out_a, out_b):
    first = lax.axis_index("core") == 0
    for part, out, take in ((part_a, out_a, jnp.logical_not(first)), (part_b, out_b, first)):
        out[...] = (part[...].astype(F32) + jnp.where(take, got[...].astype(F32), 0.0)).astype(BF)


def core_sum_kernel(mine, got, *outs):
    x = lax.axis_index("x")
    for r, out in enumerate(outs):
        k = (x + r) % 4
        out[...] = (mine[k].astype(F32) + got[k].astype(F32)).astype(BF)


def x_sum_kernel(own, p, q, r, keep, send):
    yhi = lax.axis_index("yhi")
    for out, h in ((keep, yhi), (send, 1 - yhi)):
        a, b, c, d = (part[h].astype(F32) for part in (own, p, q, r))
        out[...] = ((a + b) + (c + d)).astype(BF)


def pair_sum_kernel(a, b, out):
    out[...] = (a[...].astype(F32) + b[...].astype(F32)).astype(BF)


def quad_sum_kernel(a, b, c, d, out):
    total = (a[...].astype(F32) + b[...].astype(F32)) + (c[...].astype(F32) + d[...].astype(F32))
    out[...] = total.astype(out.dtype)


def image_out_kernel(img, a, b, c, out):
    grad = a[...].astype(F32) + (b[...].astype(F32) + c[...].astype(F32))
    out[...] = project(grad, img[...].astype(F32)).astype(BF)


def head_kernel(near, far, head, mine, other, sems):
    assemble(load_head(near, far, mine, other, sems), mine, other, head)


def text_out_kernel(z, a, b, head, out, rows, sems):
    copy = pltpu.make_async_copy(z.at[pl.ds(0, 320)], rows, sems.at[0])
    copy.start()
    grad = a[...].astype(F32) + b[...].astype(F32)
    copy.wait()
    dz = project(grad, rows[...]).astype(BF)
    out[...] = lax.dot_general(
        dz, head[...], (((1,), (1,)), ((), ())), preferred_element_type=F32
    ).astype(BF)


def apart(step, *args):
    outs = jax.eval_shape(step, *args)
    return lax.cond(
        lax.axis_index("z") < AXES["z"],
        step,
        lambda *_: jax.tree.map(lambda o: jnp.zeros(o.shape, o.dtype), outs),
        *args,
    )


hold = lax.optimization_barrier
BLOCK = shaped((320, 1152), BF)


def stack_of(*lead):
    return shaped((*lead, 72, 1152), BF)


def along_x(value):
    return lax.all_to_all(value, "x", split_axis=0, concat_axis=0, tiled=True)


def gather_head(w_h, w_y, t_log, bias):
    (pieces,) = call(repeat_kernel, [stack_of(4, 2)], [VM, VM])(w_h, w_y)
    near = along_x(pieces)
    near, t_log, bias = hold((near, t_log, bias))
    (scalars,) = call(scalar_kernel, [shaped((8, 128), F32)], [VM] * 2, flops=1 << 31)(
        t_log.reshape(1, 1), bias.reshape(1, 1)
    )
    return near, shift(near, "core", 1), scalars


def parts_of(first, shapes, *args):
    kernel = functools.partial(part_kernel, first)
    return call(kernel, shapes, [VM] * 3, flops=1 << 31)(*args)


def beside_x(part_c, scalars, grad, n_txt):
    got_c = apart_by_core(part_c)
    part_own, part_a, part_b = parts_of(0, [BLOCK] * 3, scalars, grad, n_txt)
    return part_own, *call(pass_on_kernel, [BLOCK] * 2, [VM] * 3)(part_a, part_b, got_c)


def sum_plane(scalars, mine, got_core, part_c, grad, n_txt, z, g_own, g_far, near, far):
    rel = call(core_sum_kernel, [stack_of(2)] * 4, [VM] * 2)(mine, got_core)
    got_x = [shift(rel[s], "x", s) for s in (1, 3, 2)]
    g_got = shift(g_far, "ylo", 1)
    part_own, part_a, part_b = beside_x(part_c, scalars, grad, n_txt)
    got_x[2], part_a, part_b, near, far = hold((got_x[2], part_a, part_b, near, far))
    (head,) = call(
        head_kernel,
        [shaped((1152, 1152), BF)],
        [ANY] * 2,
        [
            pltpu.VMEM((4, 2, 72, 1152), BF),
            pltpu.VMEM((4, 2, 72, 1152), BF),
            pltpu.SemaphoreType.DMA((8,)),
        ],
        flops=1 << 31,
    )(near, far)
    got_x[:2], head = hold((got_x[:2], head))
    keep, send = call(x_sum_kernel, [stack_of()] * 2, [VM] * 4)(rel[0], *got_x)
    got_a, got_b = shift(part_a, "z", -1), shift(part_b, "z", 1)
    (d_feat,) = call(
        text_out_kernel,
        [BLOCK],
        [ANY, VM, VM, VM],
        [pltpu.VMEM((320, 1152), F32), pltpu.SemaphoreType.DMA((1,))],
        flops=1 << 31,
    )(z, g_own, g_got, head)
    (one,) = call(pair_sum_kernel, [stack_of()], [VM] * 2)(keep, swap_far(send))
    (pair,) = call(pair_sum_kernel, [stack_of()], [VM] * 2)(one, shift(one, "ylo", 1))
    pair, d_feat = hold((pair, d_feat))
    return pair, d_feat, part_own, got_a, got_b


def on_device(img_emb, txt_feat, w_txt, t_log, bias):
    img, txt = img_emb[0], txt_feat[0]

    txt_far = shift(txt, "ylo", 1)
    (w_h,) = call(half_kernel, [stack_of()], [VM], vmem=60)(w_txt)
    w_y = swap_far(w_h)
    w_h, img = hold((w_h, img))
    img_c, img_b, img_a = (shift(img, "z", s) for s in (2, -1, 1))
    near, far, scalars = apart(gather_head, w_h, w_y, t_log, bias)
    near, far, txt_far = hold((near, far, txt_far))

    z, n_txt, inv = call(
        text_kernel,
        [shaped((640, 1152), F32), shaped((640, 1152), BF), shaped((640, 1), F32)],
        [ANY] * 4,
        [
            pltpu.VMEM((4, 2, 72, 1152), BF),
            pltpu.VMEM((4, 2, 72, 1152), BF),
            pltpu.VMEM((640, 1152), BF),
            pltpu.VMEM((1152, 1152), BF),
            pltpu.SemaphoreType.DMA((10,)),
        ],
        vmem=TEXT_MIB,
        flops=1 << 34,
    )(near, far, txt, txt_far)
    n_txt, img_a, img_b, img_c = hold((n_txt, img_a, img_b, img_c))
    grad, g_own, g_far, mine, other = call(
        main_kernel,
        [shaped((640, 1280), BF), BLOCK, BLOCK, stack_of(4, 2), stack_of(4, 2)],
        [VM] * 2 + [ANY] * 4 + [VM, VM, ANY, ANY],
        [
            pltpu.VMEM((1280, 1152), BF),
            pltpu.VMEM((1280, 1152), BF),
            pltpu.VMEM((640, 1152), BF),
            pltpu.VMEM((1152, 1152), F32),
            pltpu.SemaphoreType.DMA((6,)),
        ],
        vmem=MAIN_MIB,
    )(scalars, n_txt, img, img_a, img_b, img_c, z, inv, txt, txt_far)

    got_core, (part_c,) = hold(
        (shift(other, "core", 1), parts_of(3, [BLOCK], scalars, grad, n_txt))
    )
    quad, d_feat, part_own, got_a, got_b = sum_plane(
        scalars, mine, got_core, part_c, grad, n_txt, z, g_own, g_far, near, far
    )
    (d_img,) = call(image_out_kernel, [BLOCK], [VM] * 4, flops=1 << 30)(img, part_own, got_a, got_b)
    got_z = [shift(quad, "z", k) for k in (2, 1, -1)]
    got_z, d_img = hold((got_z, d_img))
    (d_weight,) = call(quad_sum_kernel, [shaped((72, 1152), F32)], [VM] * 4)(quad, *got_z)
    return (d_img[None], d_feat[None], d_weight)


def solution(mesh):
    fine = Mesh(mesh.devices.reshape(2, 4, 2, 4, 2), tuple(AXES))
    dp, fsdp = ("ylo", "z"), ("yhi", "x", "core")
    placed = (P(fsdp, dp, None), P(fsdp, dp, None), P(fsdp, None), P(), P())
    return jax.shard_map(
        on_device,
        mesh=fine,
        in_specs=placed,
        out_specs=(P(fsdp, dp, None), P(fsdp, dp, None), P(fsdp, None)),
        check_vma=False,
    )
```

```python
import functools

import jax
import jax.numpy as jnp
from jax import lax
from jax.experimental import pallas as pl
from jax.experimental.pallas import tpu as pltpu
from jax.sharding import Mesh, PartitionSpec as P

BF = jnp.bfloat16
F32 = jnp.float32
MIB = 1024 * 1024
TEXT_MIB = 14
MAIN_MIB = 28
AXES = {"ylo": 2, "z": 4, "yhi": 2, "x": 4, "core": 2}

VM = pl.BlockSpec(memory_space=pltpu.VMEM)
SM = pl.BlockSpec(memory_space=pltpu.SMEM)
ANY = pl.BlockSpec(memory_space=pl.ANY)


def shift(value, axis, step):
    n = AXES[axis]
    return lax.ppermute(value, axis, [(i, (i + step) % n) for i in range(n)])


def apart_by_core(value):
    pairs = [(z * 2 + c, (z + 1 - 2 * c) % 4 * 2 + c) for z in range(4) for c in range(2)]
    return lax.ppermute(value, ("z", "core"), pairs)


def swap_far(value):
    pairs = [(a * 2 + b, (1 - a) * 2 + 1 - b) for a in range(2) for b in range(2)]
    return lax.ppermute(value, ("ylo", "yhi"), pairs)


def shaped(shape, dtype):
    return jax.ShapeDtypeStruct(shape, dtype)


def call(kernel, outs, specs, scratch=(), vmem=10, out_specs=None, flops=1024):
    return pl.pallas_call(
        kernel,
        out_shape=outs,
        in_specs=specs,
        out_specs=out_specs or [VM] * len(outs),
        scratch_shapes=list(scratch),
        compiler_params=pltpu.CompilerParams(vmem_limit_bytes=vmem * MIB),
        cost_estimate=pl.CostEstimate(flops=flops, bytes_accessed=1024, transcendentals=0),
    )


def inverse_length(rows):
    return 1.0 / jnp.sqrt(jnp.sum(rows * rows, axis=-1, keepdims=True) + 1e-06)


def project(grad, rows, inv=None, scale=1.0):
    inv = inverse_length(rows) if inv is None else inv
    inner = jnp.sum(rows * grad, axis=-1, keepdims=True)
    return (grad - rows * (inv * inv * inner)) * (inv * scale)


def half_kernel(w, w_half):
    w_half[...] = w[...].astype(BF)


def scalar_kernel(t_log, bias, out):
    row_ids = lax.broadcasted_iota(jnp.int32, out.shape, 0)
    out[...] = jnp.where(row_ids == 0, jnp.exp(t_log[...]), bias[...])


def repeat_kernel(w_h, w_y, out):
    yhi = lax.axis_index("yhi")
    for k in range(4):
        out[k, yhi] = w_h[...]
        out[k, 1 - yhi] = w_y[...]


def load_head(near, far, mine, other, sems):
    copies = [
        pltpu.make_async_copy(src.at[x], dst.at[x], sems.at[2 * x + k])
        for x in range(4)
        for k, (src, dst) in enumerate(((near, mine), (far, other)))
    ]
    for c in copies:
        c.start()
    return copies


def assemble(copies, mine, other, head):
    core = lax.axis_index("core")
    for x in range(4):
        copies[2 * x].wait()
        copies[2 * x + 1].wait()
        for h in range(2):
            a, b = mine[x, h].astype(F32), other[x, h].astype(F32)
            first = jnp.where(core == 0, a, b)
            second = jnp.where(core == 0, b, a)
            head[pl.ds((h * 4 + x) * 144, 144), :] = jnp.concatenate([first, second], axis=0).astype(BF)


def text_kernel(near, far, txt, txt_far, z, n_txt, inv, mine, other, rows, w_full, sems):
    copies = load_head(near, far, mine, other, sems)
    late = [
        pltpu.make_async_copy(txt, rows.at[pl.ds(0, 320)], sems.at[8]),
        pltpu.make_async_copy(txt_far, rows.at[pl.ds(320, 320)], sems.at[9]),
    ]
    for c in late:
        c.start()
    assemble(copies, mine, other, w_full)
    for c in late:
        c.wait()
    out = jnp.dot(rows[...], w_full[...], preferred_element_type=F32)
    z[...] = out
    inv[...] = inverse_length(out)
    n_txt[...] = (out * inv[...]).astype(BF)


def logit_gradient(scale, bias, left, right):
    logits = scale * lax.dot_general(
        left, right, (((1,), (1,)), ((), ())), preferred_element_type=F32
    ) + bias
    return 1.0 / (1.0 + jnp.exp(-logits))


def main_kernel(scalars, n_txt, img, img_a, img_b, img_c, z, inv, txt, txt_far, grad, g_own, g_far, mine_c, other_c, mine, other, raw, rows, feat, wide, sems):
    moves = [(block, raw.at[pl.ds(k * 320, 320)]) for k, block in enumerate((img, img_a, img_b, img_c))]
    moves += [(txt, feat.at[pl.ds(0, 320)]), (txt_far, feat.at[pl.ds(320, 320)])]
    copies = [pltpu.make_async_copy(a, b, sems.at[k]) for k, (a, b) in enumerate(moves)]
    for c in copies:
        c.start()
    scale, bias = scalars[0:1, 0:1], scalars[1:2, 0:1]
    for first, last, ready in ((0, 512, copies[:2]), (512, 1280, copies[2:4])):
        for c in ready:
            c.wait()
        fresh = pl.ds(0 if first == 0 else 640, 640)
        wide_rows = raw[fresh, :].astype(F32)
        rows[fresh, :] = (wide_rows * inverse_length(wide_rows)).astype(BF)
        g = logit_gradient(scale, bias, n_txt[...], rows[pl.ds(first, last - first), :])
        grad[:, first:last] = g.astype(BF)
        if first == 0:
            own = g[:320, :384]
            row_ids = lax.broadcasted_iota(jnp.int32, own.shape, 0)
            col_ids = lax.broadcasted_iota(jnp.int32, own.shape, 1)
            grad[:320, :384] = (own - jnp.where(row_ids == col_ids, 1.0, 0.0)).astype(BF)
    parts = []
    for half, out in enumerate((g_own, g_far)):
        here = pl.ds(half * 320, 320)
        total = jnp.dot(grad[here, :], rows[...], preferred_element_type=F32)
        out[...] = (scale * total).astype(BF)
        parts.append(project(total, z[here, :], inv[here, :], scale).astype(BF))
    dz = jnp.concatenate(parts, axis=0)
    for c in copies[4:]:
        c.wait()
    wide[...] = lax.dot_general(
        feat[...], dz, (((0,), (0,)), ((), ())), preferred_element_type=F32
    )
    core, x = lax.axis_index("core"), lax.axis_index("x")
    for step in range(4):
        for h in range(2):
            chunk = h * 4 + (x + step) % 4
            own = pl.multiple_of((2 * chunk + core) * 72, 8)
            far = pl.multiple_of((2 * chunk + 1 - core) * 72, 8)
            if step == 2:
                mine_c[h] = wide[pl.ds(own, 72), :].astype(BF)
                other_c[h] = wide[pl.ds(far, 72), :].astype(BF)
            else:
                mine[min(step, 2), h] = wide[pl.ds(own, 72), :].astype(BF)
                other[min(step, 2), h] = wide[pl.ds(far, 72), :].astype(BF)


def part_kernel(first, scalars, grad, n_txt, *outs):
    start = first * 320
    rows = sum(ref.shape[0] for ref in outs)
    out = scalars[0:1, 0:1] * lax.dot_general(
        grad[:, start : start + rows], n_txt[...], (((0,), (0,)), ((), ())), preferred_element_type=F32
    )
    at = 0
    for ref in outs:
        ref[...] = out[at : at + ref.shape[0]].astype(BF)
        at += ref.shape[0]


def pass_on_kernel(part_a, part_b, got, out_a, out_b):
    first = lax.axis_index("core") == 0
    for part, out, take in ((part_a, out_a, jnp.logical_not(first)), (part_b, out_b, first)):
        out[...] = (part[...].astype(F32) + jnp.where(take, got[...].astype(F32), 0.0)).astype(BF)


def core_sum_kernel(mine, got, *outs):
    for k, out in enumerate(outs):
        out[...] = (mine[k].astype(F32) + got[k].astype(F32)).astype(BF)


def x_sum_kernel(own, p, q, r, keep, send):
    yhi = lax.axis_index("yhi")
    for out, h in ((keep, yhi), (send, 1 - yhi)):
        a, b, c, d = (part[h].astype(F32) for part in (own, p, q, r))
        out[...] = ((a + b) + (c + d)).astype(BF)


def pair_sum_kernel(a, b, out):
    out[...] = (a[...].astype(F32) + b[...].astype(F32)).astype(BF)


def quad_sum_kernel(a, b, c, d, out):
    total = (a[...].astype(F32) + b[...].astype(F32)) + (c[...].astype(F32) + d[...].astype(F32))
    out[...] = total.astype(out.dtype)


def image_out_kernel(img, a, b, c, out):
    grad = a[...].astype(F32) + (b[...].astype(F32) + c[...].astype(F32))
    out[...] = project(grad, img[...].astype(F32)).astype(BF)


def head_kernel(near, far, head, mine, other, sems):
    assemble(load_head(near, far, mine, other, sems), mine, other, head)


def text_out_kernel(z, a, b, head, out, rows, sems):
    copy = pltpu.make_async_copy(z.at[pl.ds(0, 320)], rows, sems.at[0])
    copy.start()
    grad = a[...].astype(F32) + b[...].astype(F32)
    copy.wait()
    dz = project(grad, rows[...]).astype(BF)
    out[...] = lax.dot_general(
        dz, head[...], (((1,), (1,)), ((), ())), preferred_element_type=F32
    ).astype(BF)


def apart(step, *args):
    outs = jax.eval_shape(step, *args)
    return lax.cond(
        lax.axis_index("z") < AXES["z"],
        step,
        lambda *_: jax.tree.map(lambda o: jnp.zeros(o.shape, o.dtype), outs),
        *args,
    )


hold = lax.optimization_barrier
BLOCK = shaped((320, 1152), BF)


def stack_of(*lead):
    return shaped((*lead, 72, 1152), BF)


def along_x(value):
    return lax.all_to_all(value, "x", split_axis=0, concat_axis=0, tiled=True)


def gather_head(w_h, w_y, t_log, bias):
    (pieces,) = call(repeat_kernel, [stack_of(4, 2)], [VM, VM])(w_h, w_y)
    near = along_x(pieces)
    near, t_log, bias = hold((near, t_log, bias))
    (scalars,) = call(scalar_kernel, [shaped((8, 128), F32)], [VM] * 2, flops=1 << 31)(
        t_log.reshape(1, 1), bias.reshape(1, 1)
    )
    return near, shift(near, "core", 1), scalars


def parts_of(first, shapes, *args):
    kernel = functools.partial(part_kernel, first)
    return call(kernel, shapes, [VM] * 3, flops=1 << 31)(*args)


def beside_x(part_c, scalars, grad, n_txt):
    got_c = apart_by_core(part_c)
    part_own, part_a, part_b = parts_of(0, [BLOCK] * 3, scalars, grad, n_txt)
    return part_own, *call(pass_on_kernel, [BLOCK] * 2, [VM] * 3)(part_a, part_b, got_c)


def sum_plane(scalars, mine_c, got_c, mine, got, part_c, grad, n_txt, z, g_own, g_far, near, far_core):
    (far,) = call(pair_sum_kernel, [stack_of(2)], [VM] * 2)(mine_c, got_c)
    got_x = [shift(far, "x", 2)]
    own, up, down = call(core_sum_kernel, [stack_of(2)] * 3, [VM] * 2)(mine, got)
    got_x = [shift(up, "x", 1), shift(down, "x", 3)] + got_x
    g_got = shift(g_far, "ylo", 1)
    part_own, part_a, part_b = beside_x(part_c, scalars, grad, n_txt)
    got_x[2], part_a, part_b, near, far_core = hold((got_x[2], part_a, part_b, near, far_core))
    (head,) = call(
        head_kernel,
        [shaped((1152, 1152), BF)],
        [ANY] * 2,
        [
            pltpu.VMEM((4, 2, 72, 1152), BF),
            pltpu.VMEM((4, 2, 72, 1152), BF),
            pltpu.SemaphoreType.DMA((8,)),
        ],
        flops=1 << 31,
    )(near, far_core)
    got_x[:2], head = hold((got_x[:2], head))
    keep, send = call(x_sum_kernel, [stack_of()] * 2, [VM] * 4)(own, *got_x)
    got_a, got_b = shift(part_a, "z", -1), shift(part_b, "z", 1)
    (d_feat,) = call(
        text_out_kernel,
        [BLOCK],
        [ANY, VM, VM, VM],
        [pltpu.VMEM((320, 1152), F32), pltpu.SemaphoreType.DMA((1,))],
        flops=1 << 31,
    )(z, g_own, g_got, head)
    (one,) = call(pair_sum_kernel, [stack_of()], [VM] * 2)(keep, swap_far(send))
    (pair,) = call(pair_sum_kernel, [stack_of()], [VM] * 2)(one, shift(one, "ylo", 1))
    pair, d_feat = hold((pair, d_feat))
    return pair, d_feat, part_own, got_a, got_b


def on_device(img_emb, txt_feat, w_txt, t_log, bias):
    img, txt = img_emb[0], txt_feat[0]

    txt_far = shift(txt, "ylo", 1)
    (w_h,) = call(half_kernel, [stack_of()], [VM], vmem=60)(w_txt)
    w_y = swap_far(w_h)
    w_h, img = hold((w_h, img))
    img_c, img_b, img_a = (shift(img, "z", s) for s in (2, -1, 1))
    near, far, scalars = apart(gather_head, w_h, w_y, t_log, bias)
    near, far, txt_far = hold((near, far, txt_far))

    z, n_txt, inv = call(
        text_kernel,
        [shaped((640, 1152), F32), shaped((640, 1152), BF), shaped((640, 1), F32)],
        [ANY] * 4,
        [
            pltpu.VMEM((4, 2, 72, 1152), BF),
            pltpu.VMEM((4, 2, 72, 1152), BF),
            pltpu.VMEM((640, 1152), BF),
            pltpu.VMEM((1152, 1152), BF),
            pltpu.SemaphoreType.DMA((10,)),
        ],
        vmem=TEXT_MIB,
        flops=1 << 34,
    )(near, far, txt, txt_far)
    n_txt, img_a, img_b, img_c = hold((n_txt, img_a, img_b, img_c))
    grad, g_own, g_far, mine_c, other_c, mine, other = call(
        main_kernel,
        [shaped((640, 1280), BF), BLOCK, BLOCK, stack_of(2), stack_of(2), stack_of(3, 2), stack_of(3, 2)],
        [VM] * 2 + [ANY] * 4 + [VM, VM, ANY, ANY],
        [
            pltpu.VMEM((1280, 1152), BF),
            pltpu.VMEM((1280, 1152), BF),
            pltpu.VMEM((640, 1152), BF),
            pltpu.VMEM((1152, 1152), F32),
            pltpu.SemaphoreType.DMA((6,)),
        ],
        vmem=MAIN_MIB,
    )(scalars, n_txt, img, img_a, img_b, img_c, z, inv, txt, txt_far)

    got = shift(other, "core", 1)
    got_c, (part_c,) = hold(
        (shift(other_c, "core", 1), parts_of(3, [BLOCK], scalars, grad, n_txt))
    )
    quad, d_feat, part_own, got_a, got_b = sum_plane(
        scalars, mine_c, got_c, mine, got, part_c, grad, n_txt, z, g_own, g_far, near, far
    )
    (d_img,) = call(image_out_kernel, [BLOCK], [VM] * 4, flops=1 << 30)(img, part_own, got_a, got_b)
    got_z = [shift(quad, "z", k) for k in (2, 1, -1)]
    got_z, d_img = hold((got_z, d_img))
    (d_weight,) = call(quad_sum_kernel, [shaped((72, 1152), F32)], [VM] * 4)(quad, *got_z)
    return (d_img[None], d_feat[None], d_weight)


def solution(mesh):
    fine = Mesh(mesh.devices.reshape(2, 4, 2, 4, 2), tuple(AXES))
    dp, fsdp = ("ylo", "z"), ("yhi", "x", "core")
    placed = (P(fsdp, dp, None), P(fsdp, dp, None), P(fsdp, None), P(), P())
    return jax.shard_map(
        on_device,
        mesh=fine,
        in_specs=placed,
        out_specs=(P(fsdp, dp, None), P(fsdp, dp, None), P(fsdp, None)),
        check_vma=False,
    )
```

```python
import functools

import jax
import jax.numpy as jnp
from jax import lax
from jax.experimental import pallas as pl
from jax.experimental.pallas import tpu as pltpu
from jax.sharding import Mesh, PartitionSpec as P

BF = jnp.bfloat16
F32 = jnp.float32
MIB = 1024 * 1024
TEXT_MIB = 14
MAIN_MIB = 28
AXES = {"ylo": 2, "z": 4, "yhi": 2, "x": 4, "core": 2}

VM = pl.BlockSpec(memory_space=pltpu.VMEM)
SM = pl.BlockSpec(memory_space=pltpu.SMEM)
ANY = pl.BlockSpec(memory_space=pl.ANY)


def shift(value, axis, step):
    n = AXES[axis]
    return lax.ppermute(value, axis, [(i, (i + step) % n) for i in range(n)])


def apart_by_core(value):
    pairs = [(z * 2 + c, (z + 1 - 2 * c) % 4 * 2 + c) for z in range(4) for c in range(2)]
    return lax.ppermute(value, ("z", "core"), pairs)


def swap_far(value):
    pairs = [(a * 2 + b, (1 - a) * 2 + 1 - b) for a in range(2) for b in range(2)]
    return lax.ppermute(value, ("ylo", "yhi"), pairs)


def shaped(shape, dtype):
    return jax.ShapeDtypeStruct(shape, dtype)


def call(kernel, outs, specs, scratch=(), vmem=10, out_specs=None, flops=1024):
    return pl.pallas_call(
        kernel,
        out_shape=outs,
        in_specs=specs,
        out_specs=out_specs or [VM] * len(outs),
        scratch_shapes=list(scratch),
        compiler_params=pltpu.CompilerParams(vmem_limit_bytes=vmem * MIB),
        cost_estimate=pl.CostEstimate(flops=flops, bytes_accessed=1024, transcendentals=0),
    )


def inverse_length(rows):
    return 1.0 / jnp.sqrt(jnp.sum(rows * rows, axis=-1, keepdims=True) + 1e-06)


def project(grad, rows, inv=None, scale=1.0):
    inv = inverse_length(rows) if inv is None else inv
    inner = jnp.sum(rows * grad, axis=-1, keepdims=True)
    return (grad - rows * (inv * inv * inner)) * (inv * scale)


def half_kernel(w, w_half):
    w_half[...] = w[...].astype(BF)


def scalar_kernel(t_log, bias, out):
    row_ids = lax.broadcasted_iota(jnp.int32, out.shape, 0)
    out[...] = jnp.where(row_ids == 0, jnp.exp(t_log[...]), bias[...])


def repeat_kernel(w_h, w_y, out):
    yhi = lax.axis_index("yhi")
    for k in range(4):
        out[k, yhi] = w_h[...]
        out[k, 1 - yhi] = w_y[...]


def load_head(near, far, mine, other, sems):
    copies = [
        pltpu.make_async_copy(src.at[x], dst.at[x], sems.at[2 * x + k])
        for x in range(4)
        for k, (src, dst) in enumerate(((near, mine), (far, other)))
    ]
    for c in copies:
        c.start()
    return copies


def assemble(copies, mine, other, head):
    core = lax.axis_index("core")
    for x in range(4):
        copies[2 * x].wait()
        copies[2 * x + 1].wait()
        for h in range(2):
            a, b = mine[x, h].astype(F32), other[x, h].astype(F32)
            first = jnp.where(core == 0, a, b)
            second = jnp.where(core == 0, b, a)
            head[pl.ds((h * 4 + x) * 144, 144), :] = jnp.concatenate([first, second], axis=0).astype(BF)


def text_kernel(near, far, txt, txt_far, img, z, n_txt, inv, rows, n_img, mine, other, w_full, raw, sems):
    copies = load_head(near, far, mine, other, sems)
    late = [
        pltpu.make_async_copy(txt, rows.at[pl.ds(0, 320)], sems.at[8]),
        pltpu.make_async_copy(txt_far, rows.at[pl.ds(320, 320)], sems.at[9]),
        pltpu.make_async_copy(img, raw, sems.at[10]),
    ]
    for c in late:
        c.start()
    assemble(copies, mine, other, w_full)
    for c in late:
        c.wait()
    out = jnp.dot(rows[...], w_full[...], preferred_element_type=F32)
    z[...] = out
    inv[...] = inverse_length(out)
    n_txt[...] = (out * inv[...]).astype(BF)
    own = raw[...].astype(F32)
    n_img[...] = (own * inverse_length(own)).astype(BF)


def logit_gradient(scale, bias, left, right):
    logits = scale * lax.dot_general(
        left, right, (((1,), (1,)), ((), ())), preferred_element_type=F32
    ) + bias
    return 1.0 / (1.0 + jnp.exp(-logits))


def main_kernel(scalars, n_txt, n_img, img_a, img_b, img_c, z, inv, feat, grad, g_own, g_far, mine_c, other_c, mine, other, raw, rows, wide, sems):
    moves = [(n_img, rows.at[pl.ds(0, 320)])]
    moves += [(block, raw.at[pl.ds(k * 320, 320)]) for k, block in enumerate((img_a, img_b, img_c))]
    copies = [pltpu.make_async_copy(a, b, sems.at[k]) for k, (a, b) in enumerate(moves)]
    for c in copies:
        c.start()
    scale, bias = scalars[0:1, 0:1], scalars[1:2, 0:1]
    for first, last, ready in ((0, 512, copies[:2]), (512, 1280, copies[2:4])):
        for c in ready:
            c.wait()
        begin, end = (0, 320) if first == 0 else (320, 960)
        wide_rows = raw[begin:end, :].astype(F32)
        rows[begin + 320 : end + 320, :] = (wide_rows * inverse_length(wide_rows)).astype(BF)
        g = logit_gradient(scale, bias, n_txt[...], rows[pl.ds(first, last - first), :])
        grad[:, first:last] = g.astype(BF)
        if first == 0:
            own = g[:320, :384]
            row_ids = lax.broadcasted_iota(jnp.int32, own.shape, 0)
            col_ids = lax.broadcasted_iota(jnp.int32, own.shape, 1)
            grad[:320, :384] = (own - jnp.where(row_ids == col_ids, 1.0, 0.0)).astype(BF)
    parts = []
    for half, out in enumerate((g_own, g_far)):
        here = pl.ds(half * 320, 320)
        total = jnp.dot(grad[here, :], rows[...], preferred_element_type=F32)
        out[...] = (scale * total).astype(BF)
        parts.append(project(total, z[here, :], inv[here, :], scale).astype(BF))
    dz = jnp.concatenate(parts, axis=0)
    wide[...] = lax.dot_general(
        feat[...], dz, (((0,), (0,)), ((), ())), preferred_element_type=F32
    )
    core, x = lax.axis_index("core"), lax.axis_index("x")
    for step in range(4):
        for h in range(2):
            chunk = h * 4 + (x + step) % 4
            own = pl.multiple_of((2 * chunk + core) * 72, 8)
            far = pl.multiple_of((2 * chunk + 1 - core) * 72, 8)
            if step == 2:
                mine_c[h] = wide[pl.ds(own, 72), :].astype(BF)
                other_c[h] = wide[pl.ds(far, 72), :].astype(BF)
            else:
                mine[min(step, 2), h] = wide[pl.ds(own, 72), :].astype(BF)
                other[min(step, 2), h] = wide[pl.ds(far, 72), :].astype(BF)


def part_kernel(first, scalars, grad, n_txt, *outs):
    start = first * 320
    rows = sum(ref.shape[0] for ref in outs)
    out = scalars[0:1, 0:1] * lax.dot_general(
        grad[:, start : start + rows], n_txt[...], (((0,), (0,)), ((), ())), preferred_element_type=F32
    )
    at = 0
    for ref in outs:
        ref[...] = out[at : at + ref.shape[0]].astype(BF)
        at += ref.shape[0]


def pass_on_kernel(part_a, part_b, got, out_a, out_b):
    first = lax.axis_index("core") == 0
    for part, out, take in ((part_a, out_a, jnp.logical_not(first)), (part_b, out_b, first)):
        out[...] = (part[...].astype(F32) + jnp.where(take, got[...].astype(F32), 0.0)).astype(BF)


def core_sum_kernel(mine, got, *outs):
    for k, out in enumerate(outs):
        out[...] = (mine[k].astype(F32) + got[k].astype(F32)).astype(BF)


def x_sum_kernel(own, p, q, r, keep, send):
    yhi = lax.axis_index("yhi")
    for out, h in ((keep, yhi), (send, 1 - yhi)):
        a, b, c, d = (part[h].astype(F32) for part in (own, p, q, r))
        out[...] = ((a + b) + (c + d)).astype(BF)


def pair_sum_kernel(a, b, out):
    out[...] = (a[...].astype(F32) + b[...].astype(F32)).astype(BF)


def quad_sum_kernel(a, b, c, d, out):
    total = (a[...].astype(F32) + b[...].astype(F32)) + (c[...].astype(F32) + d[...].astype(F32))
    out[...] = total.astype(out.dtype)


def image_out_kernel(img, a, b, c, out):
    grad = a[...].astype(F32) + (b[...].astype(F32) + c[...].astype(F32))
    out[...] = project(grad, img[...].astype(F32)).astype(BF)


def head_kernel(near, far, head, mine, other, sems):
    assemble(load_head(near, far, mine, other, sems), mine, other, head)


def text_out_kernel(z, a, b, head, out, rows, sems):
    copy = pltpu.make_async_copy(z.at[pl.ds(0, 320)], rows, sems.at[0])
    copy.start()
    grad = a[...].astype(F32) + b[...].astype(F32)
    copy.wait()
    dz = project(grad, rows[...]).astype(BF)
    out[...] = lax.dot_general(
        dz, head[...], (((1,), (1,)), ((), ())), preferred_element_type=F32
    ).astype(BF)


def apart(step, *args):
    outs = jax.eval_shape(step, *args)
    return lax.cond(
        lax.axis_index("z") < AXES["z"],
        step,
        lambda *_: jax.tree.map(lambda o: jnp.zeros(o.shape, o.dtype), outs),
        *args,
    )


hold = lax.optimization_barrier
BLOCK = shaped((320, 1152), BF)


def stack_of(*lead):
    return shaped((*lead, 72, 1152), BF)


def along_x(value):
    return lax.all_to_all(value, "x", split_axis=0, concat_axis=0, tiled=True)


def gather_head(w_h, w_y, t_log, bias):
    (pieces,) = call(repeat_kernel, [stack_of(4, 2)], [VM, VM])(w_h, w_y)
    near = along_x(pieces)
    near, t_log, bias = hold((near, t_log, bias))
    (scalars,) = call(scalar_kernel, [shaped((8, 128), F32)], [VM] * 2, flops=1 << 31)(
        t_log.reshape(1, 1), bias.reshape(1, 1)
    )
    return near, shift(near, "core", 1), scalars


def parts_of(first, shapes, *args):
    kernel = functools.partial(part_kernel, first)
    return call(kernel, shapes, [VM] * 3, flops=1 << 31)(*args)


def beside_x(part_c, scalars, grad, n_txt):
    got_c = apart_by_core(part_c)
    part_own, part_a, part_b = parts_of(0, [BLOCK] * 3, scalars, grad, n_txt)
    return part_own, *call(pass_on_kernel, [BLOCK] * 2, [VM] * 3)(part_a, part_b, got_c)


def sum_plane(scalars, mine_c, got_c, mine, got, part_c, grad, n_txt, z, g_own, g_far, near, far_core):
    (far,) = call(pair_sum_kernel, [stack_of(2)], [VM] * 2)(mine_c, got_c)
    got_x = [shift(far, "x", 2)]
    own, up, down = call(core_sum_kernel, [stack_of(2)] * 3, [VM] * 2)(mine, got)
    got_x = [shift(up, "x", 1), shift(down, "x", 3)] + got_x
    g_got = shift(g_far, "ylo", 1)
    part_own, part_a, part_b = beside_x(part_c, scalars, grad, n_txt)
    got_x[2], part_a, part_b, near, far_core = hold((got_x[2], part_a, part_b, near, far_core))
    (head,) = call(
        head_kernel,
        [shaped((1152, 1152), BF)],
        [ANY] * 2,
        [
            pltpu.VMEM((4, 2, 72, 1152), BF),
            pltpu.VMEM((4, 2, 72, 1152), BF),
            pltpu.SemaphoreType.DMA((8,)),
        ],
        flops=1 << 31,
    )(near, far_core)
    got_x[:2], head = hold((got_x[:2], head))
    keep, send = call(x_sum_kernel, [stack_of()] * 2, [VM] * 4)(own, *got_x)
    got_a, got_b = shift(part_a, "z", -1), shift(part_b, "z", 1)
    (d_feat,) = call(
        text_out_kernel,
        [BLOCK],
        [ANY, VM, VM, VM],
        [pltpu.VMEM((320, 1152), F32), pltpu.SemaphoreType.DMA((1,))],
        flops=1 << 31,
    )(z, g_own, g_got, head)
    (one,) = call(pair_sum_kernel, [stack_of()], [VM] * 2)(keep, swap_far(send))
    (pair,) = call(pair_sum_kernel, [stack_of()], [VM] * 2)(one, shift(one, "ylo", 1))
    pair, d_feat = hold((pair, d_feat))
    return pair, d_feat, part_own, got_a, got_b


def on_device(img_emb, txt_feat, w_txt, t_log, bias):
    img, txt = img_emb[0], txt_feat[0]

    txt_far = shift(txt, "ylo", 1)
    (w_h,) = call(half_kernel, [stack_of()], [VM], vmem=60)(w_txt)
    w_y = swap_far(w_h)
    w_h, img = hold((w_h, img))
    img_c, img_b, img_a = (shift(img, "z", s) for s in (2, -1, 1))
    near, far, scalars = apart(gather_head, w_h, w_y, t_log, bias)
    near, far, txt_far = hold((near, far, txt_far))

    z, n_txt, inv, feat, n_img = call(
        text_kernel,
        [
            shaped((640, 1152), F32),
            shaped((640, 1152), BF),
            shaped((640, 1), F32),
            shaped((640, 1152), BF),
            BLOCK,
        ],
        [ANY] * 5,
        [
            pltpu.VMEM((4, 2, 72, 1152), BF),
            pltpu.VMEM((4, 2, 72, 1152), BF),
            pltpu.VMEM((1152, 1152), BF),
            pltpu.VMEM((320, 1152), BF),
            pltpu.SemaphoreType.DMA((11,)),
        ],
        vmem=TEXT_MIB,
        flops=1 << 34,
    )(near, far, txt, txt_far, img)
    n_txt, img_a, img_b, img_c = hold((n_txt, img_a, img_b, img_c))
    grad, g_own, g_far, mine_c, other_c, mine, other = call(
        main_kernel,
        [shaped((640, 1280), BF), BLOCK, BLOCK, stack_of(2), stack_of(2), stack_of(3, 2), stack_of(3, 2)],
        [VM] * 2 + [ANY] * 4 + [VM] * 3,
        [
            pltpu.VMEM((960, 1152), BF),
            pltpu.VMEM((1280, 1152), BF),
            pltpu.VMEM((1152, 1152), F32),
            pltpu.SemaphoreType.DMA((4,)),
        ],
        vmem=MAIN_MIB,
    )(scalars, n_txt, n_img, img_a, img_b, img_c, z, inv, feat)

    got = shift(other, "core", 1)
    got_c, (part_c,) = hold(
        (shift(other_c, "core", 1), parts_of(3, [BLOCK], scalars, grad, n_txt))
    )
    quad, d_feat, part_own, got_a, got_b = sum_plane(
        scalars, mine_c, got_c, mine, got, part_c, grad, n_txt, z, g_own, g_far, near, far
    )
    (d_img,) = call(image_out_kernel, [BLOCK], [VM] * 4, flops=1 << 30)(img, part_own, got_a, got_b)
    got_z = [shift(quad, "z", k) for k in (2, 1, -1)]
    got_z, d_img = hold((got_z, d_img))
    (d_weight,) = call(quad_sum_kernel, [shaped((72, 1152), F32)], [VM] * 4)(quad, *got_z)
    return (d_img[None], d_feat[None], d_weight)


def solution(mesh):
    fine = Mesh(mesh.devices.reshape(2, 4, 2, 4, 2), tuple(AXES))
    dp, fsdp = ("ylo", "z"), ("yhi", "x", "core")
    placed = (P(fsdp, dp, None), P(fsdp, dp, None), P(fsdp, None), P(), P())
    return jax.shard_map(
        on_device,
        mesh=fine,
        in_specs=placed,
        out_specs=(P(fsdp, dp, None), P(fsdp, dp, None), P(fsdp, None)),
        check_vma=False,
    )
```

```python
import functools

import jax
import jax.numpy as jnp
from jax import lax
from jax.experimental import pallas as pl
from jax.experimental.pallas import tpu as pltpu
from jax.sharding import Mesh, PartitionSpec as P

BF = jnp.bfloat16
F32 = jnp.float32
MIB = 1024 * 1024
TEXT_MIB = 14
MAIN_MIB = 28
AXES = {"ylo": 2, "z": 4, "yhi": 2, "x": 4, "core": 2}

VM = pl.BlockSpec(memory_space=pltpu.VMEM)
SM = pl.BlockSpec(memory_space=pltpu.SMEM)
ANY = pl.BlockSpec(memory_space=pl.ANY)


def shift(value, axis, step):
    n = AXES[axis]
    return lax.ppermute(value, axis, [(i, (i + step) % n) for i in range(n)])


def apart_by_core(value):
    pairs = [(z * 2 + c, (z + 1 - 2 * c) % 4 * 2 + c) for z in range(4) for c in range(2)]
    return lax.ppermute(value, ("z", "core"), pairs)


def swap_far(value):
    pairs = [(a * 2 + b, (1 - a) * 2 + 1 - b) for a in range(2) for b in range(2)]
    return lax.ppermute(value, ("ylo", "yhi"), pairs)


def shaped(shape, dtype):
    return jax.ShapeDtypeStruct(shape, dtype)


def call(kernel, outs, specs, scratch=(), vmem=10, out_specs=None, flops=1024):
    return pl.pallas_call(
        kernel,
        out_shape=outs,
        in_specs=specs,
        out_specs=out_specs or [VM] * len(outs),
        scratch_shapes=list(scratch),
        compiler_params=pltpu.CompilerParams(vmem_limit_bytes=vmem * MIB),
        cost_estimate=pl.CostEstimate(flops=flops, bytes_accessed=1024, transcendentals=0),
    )


def inverse_length(rows):
    return 1.0 / jnp.sqrt(jnp.sum(rows * rows, axis=-1, keepdims=True) + 1e-06)


def project(grad, rows, inv=None, scale=1.0):
    inv = inverse_length(rows) if inv is None else inv
    inner = jnp.sum(rows * grad, axis=-1, keepdims=True)
    return (grad - rows * (inv * inv * inner)) * (inv * scale)


def half_kernel(w, w_half):
    w_half[...] = w[...].astype(BF)


def scalar_kernel(t_log, bias, out):
    row_ids = lax.broadcasted_iota(jnp.int32, out.shape, 0)
    out[...] = jnp.where(row_ids == 0, jnp.exp(t_log[...]), bias[...])


def repeat_kernel(w_h, w_y, out):
    yhi = lax.axis_index("yhi")
    for k in range(4):
        out[k, yhi] = w_h[...]
        out[k, 1 - yhi] = w_y[...]


def load_head(near, far, mine, other, sems):
    copies = [
        pltpu.make_async_copy(src.at[x], dst.at[x], sems.at[2 * x + k])
        for x in range(4)
        for k, (src, dst) in enumerate(((near, mine), (far, other)))
    ]
    for c in copies:
        c.start()
    return copies


def assemble(copies, mine, other, head):
    core = lax.axis_index("core")
    for x in range(4):
        copies[2 * x].wait()
        copies[2 * x + 1].wait()
        for h in range(2):
            a, b = mine[x, h].astype(F32), other[x, h].astype(F32)
            first = jnp.where(core == 0, a, b)
            second = jnp.where(core == 0, b, a)
            head[pl.ds((h * 4 + x) * 144, 144), :] = jnp.concatenate([first, second], axis=0).astype(BF)


def text_kernel(near, far, txt, txt_far, img, z, n_txt, inv, rows, n_img, mine, other, w_full, raw, sems):
    copies = load_head(near, far, mine, other, sems)
    late = [
        pltpu.make_async_copy(txt, rows.at[pl.ds(0, 320)], sems.at[8]),
        pltpu.make_async_copy(txt_far, rows.at[pl.ds(320, 320)], sems.at[9]),
        pltpu.make_async_copy(img, raw, sems.at[10]),
    ]
    for c in late:
        c.start()
    assemble(copies, mine, other, w_full)
    for c in late:
        c.wait()
    out = jnp.dot(rows[...], w_full[...], preferred_element_type=F32)
    z[...] = out
    inv[...] = inverse_length(out)
    n_txt[...] = (out * inv[...]).astype(BF)
    own = raw[...].astype(F32)
    n_img[...] = (own * inverse_length(own)).astype(BF)


def logit_gradient(scale, bias, left, right):
    logits = scale * lax.dot_general(
        left, right, (((1,), (1,)), ((), ())), preferred_element_type=F32
    ) + bias
    return 1.0 / (1.0 + jnp.exp(-logits))


def main_kernel(scalars, n_txt, n_img, img_a, img_b, img_c, z, inv, feat, grad, g_own, g_far, mine_c, other_c, mine, other, raw, rows, wide, sems):
    moves = [(n_img, rows.at[pl.ds(0, 320)])]
    moves += [(block, raw.at[pl.ds(k * 320, 320)]) for k, block in enumerate((img_a, img_b, img_c))]
    copies = [pltpu.make_async_copy(a, b, sems.at[k]) for k, (a, b) in enumerate(moves)]
    for c in copies:
        c.start()
    scale, bias = scalars[0:1, 0:1], scalars[1:2, 0:1]
    for first, last, ready in ((0, 512, copies[:2]), (512, 1280, copies[2:4])):
        for c in ready:
            c.wait()
        begin, end = (0, 320) if first == 0 else (320, 960)
        wide_rows = raw[begin:end, :].astype(F32)
        rows[begin + 320 : end + 320, :] = (wide_rows * inverse_length(wide_rows)).astype(BF)
        g = logit_gradient(scale, bias, n_txt[...], rows[pl.ds(first, last - first), :])
        grad[:, first:last] = g.astype(BF)
        if first == 0:
            own = g[:320, :384]
            row_ids = lax.broadcasted_iota(jnp.int32, own.shape, 0)
            col_ids = lax.broadcasted_iota(jnp.int32, own.shape, 1)
            grad[:320, :384] = (own - jnp.where(row_ids == col_ids, 1.0, 0.0)).astype(BF)
    parts = []
    for half, out in enumerate((g_own, g_far)):
        here = pl.ds(half * 320, 320)
        total = jnp.dot(grad[here, :], rows[...], preferred_element_type=F32)
        out[...] = (scale * total).astype(BF)
        parts.append(project(total, z[here, :], inv[here, :], scale).astype(BF))
    dz = jnp.concatenate(parts, axis=0)
    wide[...] = lax.dot_general(
        feat[...], dz, (((0,), (0,)), ((), ())), preferred_element_type=F32
    )
    core, x = lax.axis_index("core"), lax.axis_index("x")
    for step in range(4):
        for h in range(2):
            chunk = h * 4 + (x + step) % 4
            own = pl.multiple_of((2 * chunk + core) * 72, 8)
            far = pl.multiple_of((2 * chunk + 1 - core) * 72, 8)
            if step == 2:
                mine_c[h] = wide[pl.ds(own, 72), :].astype(BF)
                other_c[h] = wide[pl.ds(far, 72), :].astype(BF)
            else:
                mine[min(step, 2), h] = wide[pl.ds(own, 72), :].astype(BF)
                other[min(step, 2), h] = wide[pl.ds(far, 72), :].astype(BF)


def part_kernel(first, scalars, grad, n_txt, *outs):
    start = first * 320
    rows = sum(ref.shape[0] for ref in outs)
    out = scalars[0:1, 0:1] * lax.dot_general(
        grad[:, start : start + rows], n_txt[...], (((0,), (0,)), ((), ())), preferred_element_type=F32
    )
    at = 0
    for ref in outs:
        ref[...] = out[at : at + ref.shape[0]].astype(BF)
        at += ref.shape[0]


def pass_on_kernel(part_a, part_b, got, out_a, out_b):
    first = lax.axis_index("core") == 0
    for part, out, take in ((part_a, out_a, jnp.logical_not(first)), (part_b, out_b, first)):
        out[...] = (part[...].astype(F32) + jnp.where(take, got[...].astype(F32), 0.0)).astype(BF)


def core_sum_kernel(mine, got, *outs):
    for k, out in enumerate(outs):
        out[...] = (mine[k].astype(F32) + got[k].astype(F32)).astype(BF)


def x_sum_kernel(own, p, q, r, keep, send):
    yhi = lax.axis_index("yhi")
    for out, h in ((keep, yhi), (send, 1 - yhi)):
        a, b, c, d = (part[h].astype(F32) for part in (own, p, q, r))
        out[...] = ((a + b) + (c + d)).astype(BF)


def pair_sum_kernel(a, b, out):
    out[...] = (a[...].astype(F32) + b[...].astype(F32)).astype(BF)


def image_out_kernel(img, a, b, c, out):
    grad = a[...].astype(F32) + (b[...].astype(F32) + c[...].astype(F32))
    out[...] = project(grad, img[...].astype(F32)).astype(BF)


def head_kernel(near, far, head, mine, other, sems):
    assemble(load_head(near, far, mine, other, sems), mine, other, head)


def text_out_kernel(z, a, b, head, out, rows, sems):
    copy = pltpu.make_async_copy(z.at[pl.ds(0, 320)], rows, sems.at[0])
    copy.start()
    grad = a[...].astype(F32) + b[...].astype(F32)
    copy.wait()
    dz = project(grad, rows[...]).astype(BF)
    out[...] = lax.dot_general(
        dz, head[...], (((1,), (1,)), ((), ())), preferred_element_type=F32
    ).astype(BF)


def apart(step, *args):
    outs = jax.eval_shape(step, *args)
    return lax.cond(
        lax.axis_index("z") < AXES["z"],
        step,
        lambda *_: jax.tree.map(lambda o: jnp.zeros(o.shape, o.dtype), outs),
        *args,
    )


hold = lax.optimization_barrier
BLOCK = shaped((320, 1152), BF)


def stack_of(*lead):
    return shaped((*lead, 72, 1152), BF)


def along_x(value):
    return lax.all_to_all(value, "x", split_axis=0, concat_axis=0, tiled=True)


def gather_head(w_h, w_y, t_log, bias):
    (pieces,) = call(repeat_kernel, [stack_of(4, 2)], [VM, VM])(w_h, w_y)
    near = along_x(pieces)
    near, t_log, bias = hold((near, t_log, bias))
    (scalars,) = call(scalar_kernel, [shaped((8, 128), F32)], [VM] * 2, flops=1 << 31)(
        t_log.reshape(1, 1), bias.reshape(1, 1)
    )
    return near, shift(near, "core", 1), scalars


def parts_of(first, shapes, *args):
    kernel = functools.partial(part_kernel, first)
    return call(kernel, shapes, [VM] * 3, flops=1 << 31)(*args)


def beside_x(part_c, scalars, grad, n_txt):
    got_c = apart_by_core(part_c)
    part_own, part_a, part_b = parts_of(0, [BLOCK] * 3, scalars, grad, n_txt)
    return part_own, *call(pass_on_kernel, [BLOCK] * 2, [VM] * 3)(part_a, part_b, got_c)


def sum_plane(scalars, mine_c, got_c, mine, got, part_c, grad, n_txt, z, g_own, g_far, near, far_core):
    (far,) = call(pair_sum_kernel, [stack_of(2)], [VM] * 2)(mine_c, got_c)
    got_x = [shift(far, "x", 2)]
    own, up, down = call(core_sum_kernel, [stack_of(2)] * 3, [VM] * 2)(mine, got)
    got_x = [shift(up, "x", 1), shift(down, "x", 3)] + got_x
    g_got = shift(g_far, "ylo", 1)
    part_own, part_a, part_b = beside_x(part_c, scalars, grad, n_txt)
    got_x[2], part_a, part_b, near, far_core = hold((got_x[2], part_a, part_b, near, far_core))
    (head,) = call(
        head_kernel,
        [shaped((1152, 1152), BF)],
        [ANY] * 2,
        [
            pltpu.VMEM((4, 2, 72, 1152), BF),
            pltpu.VMEM((4, 2, 72, 1152), BF),
            pltpu.SemaphoreType.DMA((8,)),
        ],
        flops=1 << 31,
    )(near, far_core)
    got_x[:2], head = hold((got_x[:2], head))
    keep, send = call(x_sum_kernel, [stack_of()] * 2, [VM] * 4)(own, *got_x)
    got_a, got_b = shift(part_a, "z", -1), shift(part_b, "z", 1)
    (d_feat,) = call(
        text_out_kernel,
        [BLOCK],
        [ANY, VM, VM, VM],
        [pltpu.VMEM((320, 1152), F32), pltpu.SemaphoreType.DMA((1,))],
        flops=1 << 31,
    )(z, g_own, g_got, head)
    (one,) = call(pair_sum_kernel, [stack_of()], [VM] * 2)(keep, swap_far(send))
    (pair,) = call(pair_sum_kernel, [stack_of()], [VM] * 2)(one, shift(one, "ylo", 1))
    pair, d_feat = hold((pair, d_feat))
    return pair, d_feat, part_own, got_a, got_b


def on_device(img_emb, txt_feat, w_txt, t_log, bias):
    img, txt = img_emb[0], txt_feat[0]

    txt_far = shift(txt, "ylo", 1)
    (w_h,) = call(half_kernel, [stack_of()], [VM], vmem=60)(w_txt)
    w_y = swap_far(w_h)
    w_h, img = hold((w_h, img))
    img_c, img_b, img_a = (shift(img, "z", s) for s in (2, -1, 1))
    near, far, scalars = apart(gather_head, w_h, w_y, t_log, bias)
    near, far, txt_far = hold((near, far, txt_far))

    z, n_txt, inv, feat, n_img = call(
        text_kernel,
        [
            shaped((640, 1152), F32),
            shaped((640, 1152), BF),
            shaped((640, 1), F32),
            shaped((640, 1152), BF),
            BLOCK,
        ],
        [ANY] * 5,
        [
            pltpu.VMEM((4, 2, 72, 1152), BF),
            pltpu.VMEM((4, 2, 72, 1152), BF),
            pltpu.VMEM((1152, 1152), BF),
            pltpu.VMEM((320, 1152), BF),
            pltpu.SemaphoreType.DMA((11,)),
        ],
        vmem=TEXT_MIB,
        flops=1 << 34,
    )(near, far, txt, txt_far, img)
    n_txt, img_a, img_b, img_c = hold((n_txt, img_a, img_b, img_c))
    grad, g_own, g_far, mine_c, other_c, mine, other = call(
        main_kernel,
        [shaped((640, 1280), BF), BLOCK, BLOCK, stack_of(2), stack_of(2), stack_of(3, 2), stack_of(3, 2)],
        [VM] * 2 + [ANY] * 4 + [VM] * 3,
        [
            pltpu.VMEM((960, 1152), BF),
            pltpu.VMEM((1280, 1152), BF),
            pltpu.VMEM((1152, 1152), F32),
            pltpu.SemaphoreType.DMA((4,)),
        ],
        vmem=MAIN_MIB,
    )(scalars, n_txt, n_img, img_a, img_b, img_c, z, inv, feat)

    got = shift(other, "core", 1)
    got_c, (part_c,) = hold(
        (shift(other_c, "core", 1), parts_of(3, [BLOCK], scalars, grad, n_txt))
    )
    quad, d_feat, part_own, got_a, got_b = sum_plane(
        scalars, mine_c, got_c, mine, got, part_c, grad, n_txt, z, g_own, g_far, near, far
    )
    (d_img,) = call(image_out_kernel, [BLOCK], [VM] * 4, flops=1 << 30)(img, part_own, got_a, got_b)
    got_z = [shift(quad, "z", k) for k in (2, 1, -1)]
    got_z, d_img = hold((got_z, d_img))
    a, b, c, d = (v.astype(F32) for v in (quad, *got_z))
    d_weight = (a + b) + (c + d)
    return (d_img[None], d_feat[None], d_weight)


def solution(mesh):
    fine = Mesh(mesh.devices.reshape(2, 4, 2, 4, 2), tuple(AXES))
    dp, fsdp = ("ylo", "z"), ("yhi", "x", "core")
    placed = (P(fsdp, dp, None), P(fsdp, dp, None), P(fsdp, None), P(), P())
    return jax.shard_map(
        on_device,
        mesh=fine,
        in_specs=placed,
        out_specs=(P(fsdp, dp, None), P(fsdp, dp, None), P(fsdp, None)),
        check_vma=False,
    )
```
